32 devices in a mesh: dp: 2 (over x), group: 4 (over z), head: 4 (over y, core).
Axes of the slice: x: 2, y: 2, z: 4, core: 2. Of those that a mesh axis runs over, the one named last changes fastest.
Arguments:
- query: bfloat16 [1024, 2048], P('dp', ('group', 'head')), parts along dimension 0, may hold values from -200 to 200
- query_exp: int32 [64, 1024], P(('group', 'head'), 'dp'), parts along dimension 1, may hold values from -1 to 0
- kv: bfloat16 [1024, 1024], P('dp', 'group'), parts along dimension 0, may hold values from -10 to 10
- kv_exp: int32 [32, 1024], P('group', 'dp'), parts along dimension 1, may hold values from -2 to 2, as said below
- out_grad: bfloat16 [1024, 2048], P('dp', ('group', 'head')), parts along dimension 0, may hold values from -6 to 6
- out_grad_exp: int32 [64, 1024], P(('group', 'head'), 'dp'), parts along dimension 1, may hold values from -2 to 2
- q_weight: bfloat16 [4096, 2048], P('dp', ('group', 'head')), parts along dimension 0, may hold values from -0.1875 to 0.1875
- q_weight_exp: int32 [128, 2048], P('dp', ('group', 'head')), parts along dimension 0, may hold values from -1 to 1
- keyvalue_weight_mantissa: bfloat16 [4096, 1024], P(('dp', 'head'), 'group'), parts along dimension 0, may hold values from -0.375 to 0.375
- keyvalue_weight_exponent: int32 [128, 1024], P(('dp', 'head'), 'group'), parts along dimension 0, may hold values from -1 to 1
Outputs:
- input_grad: bfloat16 [1024, 2048], P(('dp', 'head'), 'group'), parts along dimension 0
- keyvalue_gradient: bfloat16 [1024, 1024], P(('dp', 'head'), 'group'), parts along dimension 0
The draws below stay inside these ranges and needn't reach their ends.
There are 2 independent parts, one for each index of `dp`. The reference program is written for one: setup_inputs(seed, part) draws one part's arguments, and reference() takes and returns one part's arrays. A program takes and returns all parts, laid end to end along the dimension named above; each array names one. Nothing has to cross between parts.
Inputs may be any that keep to these rules, and one draw needn't show every extreme that they name: `kv_exp`: exponents of the key blocks lie in -1 to 0, those of the value blocks in -2 to 2.
All inputs are finite; a program needn't handle non-finite values.
Results may differ from the reference program's by a relative error of at most 0.022.
Values may be sent and summed in bfloat16 or wider, within the bound.
A program may use at most 64 MiB of HBM per device.

```python
import jax
import jax.numpy as jnp
from jax import lax

MODEL_WIDTH = 2048
HEAD_SIZE = 128
QUERY_HEADS = 16
KEY_VALUE_HEADS = 4
SEQUENCE_TOKENS = 512


def key_block_exponents(key):
    value_section = jax.random.randint(jax.random.fold_in(key, 11), (KEY_VALUE_HEADS, 1, HEAD_SIZE // 32, SEQUENCE_TOKENS), -2, 3)
    key_section = jax.random.randint(jax.random.fold_in(key, 12), (KEY_VALUE_HEADS, 1, HEAD_SIZE // 32, SEQUENCE_TOKENS), -1, 1)
    scale_lookup = jnp.concatenate([key_section, value_section], axis=1)
    return scale_lookup.reshape(KEY_VALUE_HEADS * 2 * HEAD_SIZE // 32, SEQUENCE_TOKENS).astype(jnp.int32)


def base_keys(key):
    return jnp.clip(jax.random.normal(jax.random.fold_in(key, 13), (SEQUENCE_TOKENS, KEY_VALUE_HEADS, HEAD_SIZE), jnp.float32), -4.0, 4.0)


def draw_kv_exp(key, part):
    return key_block_exponents(key)


def draw_kv(key, part):
    keys = base_keys(key)
    value_matrix = jnp.clip(jax.random.normal(jax.random.fold_in(key, 14), (SEQUENCE_TOKENS, KEY_VALUE_HEADS, HEAD_SIZE), jnp.float32), -4.0, 4.0)
    merged_gradient = jnp.stack([keys, value_matrix], axis=2)
    return merged_gradient.reshape(SEQUENCE_TOKENS, KEY_VALUE_HEADS * 2 * HEAD_SIZE).astype(jnp.bfloat16)


def draw_query(key, part):
    base = jnp.clip(jax.random.normal(jax.random.fold_in(key, 15), (SEQUENCE_TOKENS, QUERY_HEADS, HEAD_SIZE), jnp.float32), -4.0, 4.0)
    return base.reshape(SEQUENCE_TOKENS, QUERY_HEADS * HEAD_SIZE).astype(jnp.bfloat16)


def plant(array, key, smallest, top_value):
    extent = array.shape
    index_at = [jax.random.randint(jax.random.fold_in(key, axis), (), 0, extent[axis]) for axis in range(len(extent))]
    array = array.at[tuple(index_at)].set(smallest)
    longest = extent.index(max(extent))
    index_at[longest] = (index_at[longest] + 1) % extent[longest]
    return array.at[tuple(index_at)].set(top_value)


def spiked(values, own_key, source, target, parts, factor):
    def block_of(position):
        return (jnp.arange(values.shape[position]) // (values.shape[position] // parts)).reshape((-1,) + (1,) * (values.ndim - 1 - position))

    one_side = jax.random.permutation(own_key, parts)[block_of(target)]
    far = (block_of(target) + parts // 2) % parts
    return jnp.where((block_of(source) == one_side) | (block_of(source) == far), factor * values, values)


def block_scale(stream_key, extent, shards, smallest, high):
    loudness = 1.0
    for axis_at, blocks in shards:
        heights = jax.random.uniform(jax.random.fold_in(jax.random.fold_in(stream_key, 6), axis_at), (blocks,), jnp.float32, smallest / len(shards), high / len(shards))
        loudness = loudness * jnp.repeat(jnp.exp(heights), extent[axis_at] // blocks).reshape((-1,) + (1,) * (len(extent) - 1 - axis_at))
    return loudness


def gaussian(stream_key, dims, deviation, bound, split=(), held_as=jnp.bfloat16):
    factor_of = block_scale(stream_key, dims, split, -0.22, 0.18) if split else 1.0
    values = jax.random.normal(stream_key, dims, jnp.float32) * deviation * factor_of
    return jnp.minimum(jnp.maximum(values, -bound), bound).astype(held_as)


def heavy_noise(rng, extent, deviation, limit, shards, heavy, held_as=jnp.bfloat16):
    values = deviation * jax.random.normal(rng, extent, jnp.float32)
    if shards:
        values = values * block_scale(rng, extent, shards, -0.22, 0.18)
    return jnp.clip(spiked(values, jax.random.fold_in(rng, 3), *heavy), -limit, limit).astype(held_as)


def setup_inputs(seed: int = 0, part: int = 0) -> dict:
    arg_keys = jax.random.split(jax.random.key(seed), 11)
    part_keys = jax.random.split(jax.random.fold_in(arg_keys[10], part), 11)
    return {
        "query": draw_query(jax.random.fold_in(jax.random.fold_in(arg_keys[10], part), 71), part),
        "query_exp": plant(jax.random.randint(part_keys[1], (QUERY_HEADS * HEAD_SIZE // 32, SEQUENCE_TOKENS), -1, 1), jax.random.fold_in(part_keys[1], 1), -1, 0).astype(jnp.int32),
        "kv": draw_kv(jax.random.fold_in(jax.random.fold_in(arg_keys[10], part), 71), part),
        "kv_exp": draw_kv_exp(jax.random.fold_in(jax.random.fold_in(arg_keys[10], part), 71), part),
        "out_grad": gaussian(part_keys[4], (SEQUENCE_TOKENS, QUERY_HEADS * HEAD_SIZE), 1.0, 6.0, ((1, 16),)),
        "out_grad_exp": plant(jax.random.randint(part_keys[5], (QUERY_HEADS * HEAD_SIZE // 32, SEQUENCE_TOKENS), -2, 3), jax.random.fold_in(part_keys[5], 1), -2, 2).astype(jnp.int32),
        "q_weight": heavy_noise(part_keys[6], (MODEL_WIDTH, QUERY_HEADS * HEAD_SIZE), (QUERY_HEADS * HEAD_SIZE) ** -0.5, 0.1875, ((1, 16),), (1, 0, 16, 2.0)),
        "q_weight_exp": plant(jax.random.randint(part_keys[7], (MODEL_WIDTH // 32, QUERY_HEADS * HEAD_SIZE), -1, 2), jax.random.fold_in(part_keys[7], 1), -1, 1).astype(jnp.int32),
        "keyvalue_weight_mantissa": gaussian(part_keys[8], (MODEL_WIDTH, KEY_VALUE_HEADS * 2 * HEAD_SIZE), (2 * HEAD_SIZE) ** -0.5, 0.375, ((0, 4), (1, 4))),
        "keyvalue_weight_exponent": plant(jax.random.randint(part_keys[9], (MODEL_WIDTH // 32, KEY_VALUE_HEADS * 2 * HEAD_SIZE), -1, 2), jax.random.fold_in(part_keys[9], 1), -1, 1).astype(jnp.int32),
    }


def power_of_two(block_exponent):
    scale_lookup = jnp.zeros(block_exponent.shape, jnp.float32)
    for level in range(-4, 5):
        scale_lookup = scale_lookup + jnp.where(block_exponent == level, 2.0 ** level, 0.0).astype(jnp.float32)
    return scale_lookup


def dequant_rows(mantissa, block_exponent):
    scaling = jnp.repeat(power_of_two(block_exponent).T, 32, axis=1)
    return (mantissa.astype(jnp.float32) * scaling).astype(jnp.bfloat16)


def dequant_cols(mantissa, block_exponent):
    scaling = jnp.repeat(power_of_two(block_exponent), 32, axis=0)
    return (mantissa.astype(jnp.float32) * scaling).astype(jnp.bfloat16)


def reference(query, query_exp, kv, kv_exp, out_grad, out_grad_exp, q_weight, q_weight_exp, keyvalue_weight_mantissa, keyvalue_weight_exponent):
    scale = 1.0 / (HEAD_SIZE ** 0.5)
    q_full = dequant_rows(query, query_exp)
    keyvalue_dense = dequant_rows(kv, kv_exp)
    do_full = dequant_rows(out_grad, out_grad_exp)
    heads_q = q_full.reshape(SEQUENCE_TOKENS, QUERY_HEADS, HEAD_SIZE).transpose(1, 0, 2)
    heads_do = do_full.reshape(SEQUENCE_TOKENS, QUERY_HEADS, HEAD_SIZE).transpose(1, 0, 2)
    keyvalue_head_list = keyvalue_dense.reshape(SEQUENCE_TOKENS, KEY_VALUE_HEADS, 2, HEAD_SIZE).transpose(1, 2, 0, 3)
    heads_per_group = QUERY_HEADS // KEY_VALUE_HEADS
    rows = jnp.arange(SEQUENCE_TOKENS, dtype=jnp.int32)
    visible = rows[None, :] <= rows[:, None]

    def one_head(item):
        q_head, do_head, number = item
        group_id = number // heads_per_group
        keys = keyvalue_head_list[group_id, 0]
        value_matrix = keyvalue_head_list[group_id, 1]
        scores = lax.dot_general(q_head, keys, (((1,), (1,)), ((), ())), preferred_element_type=jnp.float32) * scale
        scores = jnp.where(visible, scores, -jnp.inf)
        peak = jnp.max(scores, axis=1, keepdims=True)
        expd = jnp.exp(scores - peak)
        probs = expd / jnp.sum(expd, axis=1, keepdims=True)
        probs_b = probs.astype(jnp.bfloat16)
        output = jnp.dot(probs_b, value_matrix, preferred_element_type=jnp.float32)
        delta = jnp.sum(do_head.astype(jnp.float32) * output, axis=1, keepdims=True)
        dprob = lax.dot_general(do_head, value_matrix, (((1,), (1,)), ((), ())), preferred_element_type=jnp.float32)
        dscore = (probs * (dprob - delta) * scale).astype(jnp.bfloat16)
        dq_head = jnp.dot(dscore, keys, preferred_element_type=jnp.float32).astype(jnp.bfloat16)
        dk_head = lax.dot_general(dscore, q_head, (((0,), (0,)), ((), ())), preferred_element_type=jnp.float32).astype(jnp.bfloat16)
        dv_head = lax.dot_general(probs_b, do_head, (((0,), (0,)), ((), ())), preferred_element_type=jnp.float32).astype(jnp.bfloat16)
        return dq_head, dk_head, dv_head

    dq_all, key_gradient_full, value_gradient_full = lax.map(one_head, (heads_q, heads_do, jnp.arange(QUERY_HEADS, dtype=jnp.int32)))
    key_gradient_total = jnp.sum(key_gradient_full.astype(jnp.float32).reshape(KEY_VALUE_HEADS, heads_per_group, SEQUENCE_TOKENS, HEAD_SIZE), axis=1)
    value_gradient_total = jnp.sum(value_gradient_full.astype(jnp.float32).reshape(KEY_VALUE_HEADS, heads_per_group, SEQUENCE_TOKENS, HEAD_SIZE), axis=1)
    keyvalue_gradient = jnp.stack([key_gradient_total, value_gradient_total], axis=1).transpose(2, 0, 1, 3).reshape(SEQUENCE_TOKENS, KEY_VALUE_HEADS * 2 * HEAD_SIZE).astype(jnp.bfloat16)
    dq_rows = dq_all.transpose(1, 0, 2).reshape(SEQUENCE_TOKENS, QUERY_HEADS * HEAD_SIZE)
    w_query = dequant_cols(q_weight, q_weight_exp)
    w_keyval = dequant_cols(keyvalue_weight_mantissa, keyvalue_weight_exponent)
    total = lax.dot_general(dq_rows, w_query, (((1,), (1,)), ((), ())), preferred_element_type=jnp.float32)
    total = total + lax.dot_general(keyvalue_gradient, w_keyval, (((1,), (1,)), ((), ())), preferred_element_type=jnp.float32)
    return total.astype(jnp.bfloat16), keyvalue_gradient
```

```python
import functools

import jax
import jax.numpy as jnp
from jax import lax
from jax.experimental import pallas as pl
from jax.experimental.pallas import tpu as pltpu
from jax.sharding import PartitionSpec as P

MESH = pl.DeviceIdType.MESH
F32 = jnp.float32
BF16 = jnp.bfloat16
CORES = 2
BLOCK = 32


def power_of_two(exponent):
    scale = jnp.where(exponent == 0, 1.0, 0.0)
    for level in (-4, -3, -2, -1, 1, 2, 3, 4):
        scale = jnp.where(exponent == level, 2.0**level, scale)
    return scale.astype(F32)


def dequant_rows(mantissa, exponent):
    blocks, rows = exponent.shape
    scale = jnp.broadcast_to(power_of_two(exponent)[:, None, :], (blocks, BLOCK, rows))
    scale = scale.reshape(blocks * BLOCK, rows).T
    return (mantissa.astype(F32) * scale).astype(BF16)


def dequant_cols(mantissa, exponent):
    blocks, columns = exponent.shape
    scale = jnp.broadcast_to(power_of_two(exponent)[:, None, :], (blocks, BLOCK, columns))
    return (mantissa.astype(F32) * scale.reshape(blocks * BLOCK, columns)).astype(BF16)


def dot_nt(a, b):
    return lax.dot_general(a, b, (((1,), (1,)), ((), ())), preferred_element_type=F32)


def dot_tn(a, b):
    return lax.dot_general(a, b, (((0,), (0,)), ((), ())), preferred_element_type=F32)


def kernel(
    groups,
    heads,
    q_ref,
    qe_ref,
    kv_ref,
    kve_ref,
    do_ref,
    doe_ref,
    wq_ref,
    wqe_ref,
    wkv_ref,
    wkve_ref,
    out_ref,
    kvg_ref,
    wq_pair,
    wq_out,
    wkv_half,
    wkv_out,
    dq_pair,
    dkv_out,
    dkv_in,
    kvg_pair,
    part_out,
    part_in,
    z_out,
    z_in,
    dk_acc,
    dv_acc,
    w_sem,
    wkv_send,
    wkv_recv,
    dq_sem,
    dkv_send,
    dkv_recv,
    kvg_sem,
    part_send,
    part_recv,
    z_send,
    z_recv,
):
    seq, size = q_ref.shape
    model = wq_ref.shape[0]
    chips = heads // CORES
    tokens = seq // heads
    wide = model // groups
    half = model // CORES
    per_half = groups // CORES
    rows = wkv_ref.shape[0]
    owners = heads // CORES
    scale = 1.0 / size**0.5

    z = lax.axis_index("group")
    h = lax.axis_index("head")
    y = h // CORES
    c = lax.rem(h, CORES)
    sibling = y * CORES + (1 - c)

    barrier = pltpu.get_barrier_semaphore()
    for k in range(1, heads):
        pl.semaphore_signal(
            barrier, inc=1, device_id={"head": lax.rem(h + k, heads)}, device_id_type=MESH
        )
    for k in range(1, groups):
        for core in range(CORES):
            pl.semaphore_signal(
                barrier,
                inc=1,
                device_id={"group": lax.rem(z + k, groups), "head": y * CORES + core},
                device_id_type=MESH,
            )

    def weight_rows(which):
        first = pl.multiple_of(which * half, half)
        first_e = pl.multiple_of(which * (half // BLOCK), half // BLOCK)
        return dequant_cols(
            wq_ref[pl.ds(first, half), :], wqe_ref[pl.ds(first_e, half // BLOCK), :]
        )

    wq_out[...] = weight_rows(1 - c)
    wkv_out[...] = dequant_cols(wkv_ref[...], wkve_ref[...])
    pl.semaphore_wait(barrier, heads - 1 + CORES * (groups - 1))

    my_half = h // owners
    my_slot = pl.multiple_of(lax.rem(h, owners) * rows, rows)

    def wkv_copy(j):
        return pltpu.make_async_remote_copy(
            src_ref=wkv_out,
            dst_ref=wkv_half.at[pl.ds(my_slot, rows)],
            send_sem=wkv_send.at[j],
            recv_sem=wkv_recv.at[lax.rem(h, owners)],
            device_id={"head": CORES * j + my_half},
            device_id_type=MESH,
        )

    for j in range(owners):

        @pl.when(CORES * j + my_half != h)
        def _():
            wkv_copy(j).start()

    w_copy = pltpu.make_async_remote_copy(
        src_ref=wq_out,
        dst_ref=wq_pair.at[:, size:],
        send_sem=w_sem.at[0],
        recv_sem=w_sem.at[1],
        device_id={"head": sibling},
        device_id_type=MESH,
    )
    w_copy.start()
    wq_pair[:, :size] = weight_rows(c)

    @pl.when(my_half == c)
    def _():
        wkv_half[pl.ds(my_slot, rows), :] = wkv_out[...]

    query = dequant_rows(q_ref[...], qe_ref[...])
    kv = dequant_rows(kv_ref[...], kve_ref[...])
    grad = dequant_rows(do_ref[...], doe_ref[...])
    keys, values = kv[:, :size], kv[:, size:]
    block = min(256, seq)
    for index in reversed(range(seq // block)):
        first, upper = index * block, (index + 1) * block
        q_block, do_block = query[first:upper], grad[first:upper]
        scores = dot_nt(keys[:upper], q_block)
        key_at = lax.broadcasted_iota(jnp.int32, (upper, block), 0)
        query_at = first + lax.broadcasted_iota(jnp.int32, (upper, block), 1)
        scores = jnp.where(key_at <= query_at, scores, -jnp.inf)
        expd = jnp.exp((scores - jnp.max(scores, axis=0, keepdims=True)) * scale)
        probs = expd * (1.0 / jnp.sum(expd, axis=0, keepdims=True))
        probs_b = probs.astype(BF16)
        dprob = dot_nt(values[:upper], do_block)
        delta = jnp.sum(probs_b.astype(F32) * dprob, axis=0, keepdims=True)
        dscore = (probs * (dprob - delta) * scale).astype(BF16)
        dq_pair[first:upper, :size] = dot_tn(dscore, keys[:upper]).astype(BF16)
        dk = jnp.dot(dscore, q_block, preferred_element_type=F32)
        dv = jnp.dot(probs_b, do_block, preferred_element_type=F32)
        if upper == seq:
            dk_acc[...] = dk
            dv_acc[...] = dv
        else:
            dk_acc[:upper, :] += dk
            dv_acc[:upper, :] += dv

    dq_copy = pltpu.make_async_remote_copy(
        src_ref=dq_pair.at[:, :size],
        dst_ref=dq_pair.at[:, size:],
        send_sem=dq_sem.at[0],
        recv_sem=dq_sem.at[1],
        device_id={"head": sibling},
        device_id_type=MESH,
    )
    dq_copy.start()
    dkv_out[:, :size] = dk_acc[...].astype(BF16)
    dkv_out[:, size:] = dv_acc[...].astype(BF16)
    dkv_copies = []
    for k in range(1, heads):
        to = lax.rem(h + k, heads)
        copy = pltpu.make_async_remote_copy(
            src_ref=dkv_out.at[pl.ds(pl.multiple_of(to * tokens, tokens), tokens)],
            dst_ref=dkv_in.at[k - 1],
            send_sem=dkv_send.at[k - 1],
            recv_sem=dkv_recv.at[k - 1],
            device_id={"head": to},
            device_id_type=MESH,
        )
        copy.start()
        dkv_copies.append(copy)

    def q_term(chip, b, core):
        first = pl.multiple_of((chip * CORES + core) * tokens, tokens)
        at = pl.multiple_of(b * wide, wide)
        return dot_nt(dq_pair[pl.ds(first, tokens), :], wq_pair[pl.ds(at, wide), :])

    w_copy.wait_recv()
    dq_copy.wait_recv()
    chunks = [(i, core) for i in range(per_half) for core in range(CORES)]
    part_copies = {}
    for i, core in chunks:
        b = lax.rem(z + 1 + i, per_half)
        for k in range(1, chips):
            to = lax.rem(y + k, chips)
            part_out[k - 1, i, core] = q_term(to, b, core).astype(BF16)
            copy = pltpu.make_async_remote_copy(
                src_ref=part_out.at[k - 1, i, core],
                dst_ref=part_in.at[k - 1, i, core],
                send_sem=part_send.at[k - 1, i, core],
                recv_sem=part_recv.at[k - 1, i, core],
                device_id={"head": to * CORES + c},
                device_id_type=MESH,
            )
            copy.start()
            part_copies[k, i, core] = copy

    total = dkv_out[pl.ds(pl.multiple_of(h * tokens, tokens), tokens), :].astype(F32)
    for k in range(1, heads):
        dkv_copies[k - 1].wait_recv()
        total = total + dkv_in[k - 1].astype(F32)
    kvg = total.astype(BF16)
    kvg_ref[...] = kvg
    kvg_pair[c] = kvg
    kvg_copy = pltpu.make_async_remote_copy(
        src_ref=kvg_pair.at[c],
        dst_ref=kvg_pair.at[c],
        send_sem=kvg_sem.at[0],
        recv_sem=kvg_sem.at[1],
        device_id={"head": sibling},
        device_id_type=MESH,
    )
    kvg_copy.start()
    for s in range(owners):

        @pl.when(c * owners + s != h)
        def _():
            pltpu.make_async_remote_copy(
                src_ref=wkv_out,
                dst_ref=wkv_half.at[pl.ds(s * rows, rows)],
                send_sem=wkv_send.at[s],
                recv_sem=wkv_recv.at[s],
                device_id={"head": sibling},
                device_id_type=MESH,
            ).wait_recv()

    pltpu.make_async_remote_copy(
        src_ref=kvg_pair.at[c],
        dst_ref=kvg_pair.at[1 - c],
        send_sem=kvg_sem.at[0],
        recv_sem=kvg_sem.at[1],
        device_id={"head": sibling},
        device_id_type=MESH,
    ).wait_recv()

    def z_copy(i, core, to_z, head):
        return pltpu.make_async_remote_copy(
            src_ref=z_out.at[i, core],
            dst_ref=z_in.at[z],
            send_sem=z_send.at[i, core],
            recv_sem=z_recv.at[z],
            device_id={"group": to_z, "head": head},
            device_id_type=MESH,
        )

    for i, core in chunks:
        b = lax.rem(z + 1 + i, per_half)
        to_z = c * per_half + b
        at = pl.multiple_of(b * wide, wide)
        acc = q_term(y, b, core)
        acc = acc + dot_nt(kvg_pair[core], wkv_half[pl.ds(at, wide), :])
        for k in range(1, chips):
            part_copies[k, i, core].wait_recv()
            acc = acc + part_in[k - 1, i, core].astype(F32)
        z_out[i, core] = acc.astype(BF16)
        away = jnp.logical_or(to_z != z, core != c)

        @pl.when(away)
        def _():
            z_copy(i, core, to_z, y * CORES + core).start()

        @pl.when(jnp.logical_not(away))
        def _():
            z_in[z] = z_out[i, core]

    source_core = z // per_half
    result = None
    for source in range(groups):

        @pl.when(jnp.logical_or(source != z, source_core != c))
        def _():
            pltpu.make_async_remote_copy(
                src_ref=z_out.at[0, 0],
                dst_ref=z_in.at[source],
                send_sem=z_send.at[0, 0],
                recv_sem=z_recv.at[source],
                device_id={"head": sibling},
                device_id_type=MESH,
            ).wait_recv()

        term = z_in[source].astype(F32)
        result = term if result is None else result + term
    out_ref[...] = result.astype(BF16)

    for j in range(owners):

        @pl.when(CORES * j + my_half != h)
        def _():
            wkv_copy(j).wait_send()

    for copy in [w_copy, dq_copy, kvg_copy, *dkv_copies, *part_copies.values()]:
        copy.wait_send()
    for i, core in chunks:
        to_z = c * per_half + lax.rem(z + 1 + i, per_half)

        @pl.when(jnp.logical_or(to_z != z, core != c))
        def _():
            z_copy(i, core, to_z, y * CORES + core).wait_send()


def shards(groups, heads, *args):
    query, kv, q_weight, kv_weight = args[0], args[2], args[6], args[8]
    seq, size = query.shape
    model = q_weight.shape[0]
    chips = heads // CORES
    tokens = seq // heads
    wide = model // groups
    half = model // CORES
    per_half = groups // CORES
    owners = heads // CORES
    dma = pltpu.SemaphoreType.DMA
    vmem = pl.BlockSpec(memory_space=pltpu.VMEM)
    return pl.pallas_call(
        functools.partial(kernel, groups, heads),
        out_shape=(
            jax.ShapeDtypeStruct((tokens, wide), BF16),
            jax.ShapeDtypeStruct((tokens, 2 * size), BF16),
        ),
        in_specs=[vmem] * len(args),
        out_specs=(vmem, vmem),
        scratch_shapes=[
            pltpu.VMEM((half, 2 * size), BF16),
            pltpu.VMEM((half, size), BF16),
            pltpu.VMEM((half, 2 * size), BF16),
            pltpu.VMEM(kv_weight.shape, BF16),
            pltpu.VMEM((seq, 2 * size), BF16),
            pltpu.VMEM((seq, 2 * size), BF16),
            pltpu.VMEM((heads - 1, tokens, 2 * size), BF16),
            pltpu.VMEM((CORES, tokens, 2 * size), BF16),
            pltpu.VMEM((chips - 1, per_half, CORES, tokens, wide), BF16),
            pltpu.VMEM((chips - 1, per_half, CORES, tokens, wide), BF16),
            pltpu.VMEM((per_half, CORES, tokens, wide), BF16),
            pltpu.VMEM((groups, tokens, wide), BF16),
            pltpu.VMEM((seq, size), F32),
            pltpu.VMEM((seq, size), F32),
            dma((2,)),
            dma((owners,)),
            dma((owners,)),
            dma((2,)),
            dma((heads - 1,)),
            dma((heads - 1,)),
            dma((2,)),
            dma((chips - 1, per_half, CORES)),
            dma((chips - 1, per_half, CORES)),
            dma((per_half, CORES)),
            dma((groups,)),
        ],
        compiler_params=pltpu.CompilerParams(
            collective_id=0, has_side_effects=True, vmem_limit_bytes=48 * 1024 * 1024
        ),
    )(*args)


def solution(mesh):
    return jax.shard_map(
        functools.partial(shards, mesh.shape["group"], mesh.shape["head"]),
        mesh=mesh,
        in_specs=(
            P("dp", ("group", "head")),
            P(("group", "head"), "dp"),
            P("dp", "group"),
            P("group", "dp"),
            P("dp", ("group", "head")),
            P(("group", "head"), "dp"),
            P("dp", ("group", "head")),
            P("dp", ("group", "head")),
            P(("dp", "head"), "group"),
            P(("dp", "head"), "group"),
        ),
        out_specs=(P(("dp", "head"), "group"), P(("dp", "head"), "group")),
        check_vma=False,
    )
```

```python
import functools

import jax
import jax.numpy as jnp
from jax import lax
from jax.experimental import pallas as pl
from jax.experimental.pallas import tpu as pltpu
from jax.sharding import PartitionSpec as P

MESH = pl.DeviceIdType.MESH
F32 = jnp.float32
BF16 = jnp.bfloat16
CORES = 2
BLOCK = 32
ARGS = 10
LOAD_ORDER = (8, 9, 6, 7, 0, 1, 2, 3, 4, 5)


def power_of_two(exponent):
    scale = jnp.where(exponent == 0, 1.0, 0.0)
    for level in (-4, -3, -2, -1, 1, 2, 3, 4):
        scale = jnp.where(exponent == level, 2.0**level, scale)
    return scale.astype(F32)


def dequant_rows(mantissa, exponent):
    blocks, rows = exponent.shape
    scale = jnp.broadcast_to(power_of_two(exponent)[:, None, :], (blocks, BLOCK, rows))
    scale = scale.reshape(blocks * BLOCK, rows).T
    return (mantissa.astype(F32) * scale).astype(BF16)


def dequant_cols(mantissa, exponent):
    blocks, columns = exponent.shape
    scale = jnp.broadcast_to(power_of_two(exponent)[:, None, :], (blocks, BLOCK, columns))
    return (mantissa.astype(F32) * scale.reshape(blocks * BLOCK, columns)).astype(BF16)


def dot_nt(a, b):
    return lax.dot_general(a, b, (((1,), (1,)), ((), ())), preferred_element_type=F32)


def dot_tn(a, b):
    return lax.dot_general(a, b, (((0,), (0,)), ((), ())), preferred_element_type=F32)


def kernel(
    groups,
    heads,
    *refs,
):
    sources, (out_ref, kvg_ref) = refs[:ARGS], refs[ARGS : ARGS + 2]
    held = refs[ARGS + 2 : 2 * ARGS + 2]
    q_ref, qe_ref, kv_ref, kve_ref, do_ref, doe_ref, wq_ref, wqe_ref, wkv_ref, wkve_ref = held
    (
        load_sem,
        wq_pair,
        wq_out,
        wkv_half,
        wkv_out,
        dq_pair,
        dkv_out,
        dkv_in,
        kvg_pair,
        part_out,
        part_in,
        z_out,
        z_in,
        dk_acc,
        dv_acc,
        w_sem,
        wkv_send,
        wkv_recv,
        dq_sem,
        dkv_send,
        dkv_recv,
        kvg_sem,
        part_send,
        part_recv,
        z_send,
        z_recv,
    ) = refs[2 * ARGS + 2 :]
    seq, size = q_ref.shape
    model = wq_ref.shape[0]
    chips = heads // CORES
    tokens = seq // heads
    wide = model // groups
    half = model // CORES
    per_half = groups // CORES
    rows = wkv_ref.shape[0]
    owners = heads // CORES
    scale = 1.0 / size**0.5

    z = lax.axis_index("group")
    h = lax.axis_index("head")
    y = h // CORES
    c = lax.rem(h, CORES)
    sibling = y * CORES + (1 - c)

    loads = [
        pltpu.make_async_copy(source, held[at], load_sem.at[at])
        for at, source in enumerate(sources)
    ]
    for at in LOAD_ORDER:
        loads[at].start()

    barrier = pltpu.get_barrier_semaphore()
    for k in range(1, heads):
        pl.semaphore_signal(
            barrier, inc=1, device_id={"head": lax.rem(h + k, heads)}, device_id_type=MESH
        )
    for k in range(1, groups):
        for core in range(CORES):
            pl.semaphore_signal(
                barrier,
                inc=1,
                device_id={"group": lax.rem(z + k, groups), "head": y * CORES + core},
                device_id_type=MESH,
            )

    def weight_rows(which):
        first = pl.multiple_of(which * half, half)
        first_e = pl.multiple_of(which * (half // BLOCK), half // BLOCK)
        return dequant_cols(
            wq_ref[pl.ds(first, half), :], wqe_ref[pl.ds(first_e, half // BLOCK), :]
        )

    for at in LOAD_ORDER[:4]:
        loads[at].wait()
    wq_out[...] = weight_rows(1 - c)
    wkv_out[...] = dequant_cols(wkv_ref[...], wkve_ref[...])
    pl.semaphore_wait(barrier, heads - 1 + CORES * (groups - 1))

    my_half = h // owners
    my_slot = pl.multiple_of(lax.rem(h, owners) * rows, rows)

    def wkv_copy(j):
        return pltpu.make_async_remote_copy(
            src_ref=wkv_out,
            dst_ref=wkv_half.at[pl.ds(my_slot, rows)],
            send_sem=wkv_send.at[j],
            recv_sem=wkv_recv.at[lax.rem(h, owners)],
            device_id={"head": CORES * j + my_half},
            device_id_type=MESH,
        )

    for j in range(owners):

        @pl.when(CORES * j + my_half != h)
        def _():
            wkv_copy(j).start()

    w_copy = pltpu.make_async_remote_copy(
        src_ref=wq_out,
        dst_ref=wq_pair.at[:, size:],
        send_sem=w_sem.at[0],
        recv_sem=w_sem.at[1],
        device_id={"head": sibling},
        device_id_type=MESH,
    )
    w_copy.start()
    wq_pair[:, :size] = weight_rows(c)

    @pl.when(my_half == c)
    def _():
        wkv_half[pl.ds(my_slot, rows), :] = wkv_out[...]

    for at in LOAD_ORDER[4:]:
        loads[at].wait()
    query = dequant_rows(q_ref[...], qe_ref[...])
    kv = dequant_rows(kv_ref[...], kve_ref[...])
    grad = dequant_rows(do_ref[...], doe_ref[...])
    keys, values = kv[:, :size], kv[:, size:]
    block = min(256, seq)
    for index in reversed(range(seq // block)):
        first, upper = index * block, (index + 1) * block
        q_block, do_block = query[first:upper], grad[first:upper]
        scores = dot_nt(keys[:upper], q_block)
        key_at = lax.broadcasted_iota(jnp.int32, (upper, block), 0)
        query_at = first + lax.broadcasted_iota(jnp.int32, (upper, block), 1)
        scores = jnp.where(key_at <= query_at, scores, -jnp.inf)
        expd = jnp.exp((scores - jnp.max(scores, axis=0, keepdims=True)) * scale)
        probs = expd * (1.0 / jnp.sum(expd, axis=0, keepdims=True))
        probs_b = probs.astype(BF16)
        dprob = dot_nt(values[:upper], do_block)
        delta = jnp.sum(probs_b.astype(F32) * dprob, axis=0, keepdims=True)
        dscore = (probs * (dprob - delta) * scale).astype(BF16)
        dq_pair[first:upper, :size] = dot_tn(dscore, keys[:upper]).astype(BF16)
        dk = jnp.dot(dscore, q_block, preferred_element_type=F32)
        dv = jnp.dot(probs_b, do_block, preferred_element_type=F32)
        if upper == seq:
            dk_acc[...] = dk
            dv_acc[...] = dv
        else:
            dk_acc[:upper, :] += dk
            dv_acc[:upper, :] += dv

    dq_copy = pltpu.make_async_remote_copy(
        src_ref=dq_pair.at[:, :size],
        dst_ref=dq_pair.at[:, size:],
        send_sem=dq_sem.at[0],
        recv_sem=dq_sem.at[1],
        device_id={"head": sibling},
        device_id_type=MESH,
    )
    dq_copy.start()
    dkv_out[:, :size] = dk_acc[...].astype(BF16)
    dkv_out[:, size:] = dv_acc[...].astype(BF16)
    dkv_copies = []
    for k in range(1, heads):
        to = lax.rem(h + k, heads)
        copy = pltpu.make_async_remote_copy(
            src_ref=dkv_out.at[pl.ds(pl.multiple_of(to * tokens, tokens), tokens)],
            dst_ref=dkv_in.at[k - 1],
            send_sem=dkv_send.at[k - 1],
            recv_sem=dkv_recv.at[k - 1],
            device_id={"head": to},
            device_id_type=MESH,
        )
        copy.start()
        dkv_copies.append(copy)

    def q_term(chip, b, core):
        first = pl.multiple_of((chip * CORES + core) * tokens, tokens)
        at = pl.multiple_of(b * wide, wide)
        return dot_nt(dq_pair[pl.ds(first, tokens), :], wq_pair[pl.ds(at, wide), :])

    w_copy.wait_recv()
    dq_copy.wait_recv()
    chunks = [(i, core) for i in range(per_half) for core in range(CORES)]
    part_copies = {}
    for i, core in chunks:
        b = lax.rem(z + 1 + i, per_half)
        for k in range(1, chips):
            to = lax.rem(y + k, chips)
            part_out[k - 1, i, core] = q_term(to, b, core).astype(BF16)
            copy = pltpu.make_async_remote_copy(
                src_ref=part_out.at[k - 1, i, core],
                dst_ref=part_in.at[k - 1, i, core],
                send_sem=part_send.at[k - 1, i, core],
                recv_sem=part_recv.at[k - 1, i, core],
                device_id={"head": to * CORES + c},
                device_id_type=MESH,
            )
            copy.start()
            part_copies[k, i, core] = copy

    total = dkv_out[pl.ds(pl.multiple_of(h * tokens, tokens), tokens), :].astype(F32)
    for k in range(1, heads):
        dkv_copies[k - 1].wait_recv()
        total = total + dkv_in[k - 1].astype(F32)
    kvg = total.astype(BF16)
    kvg_ref[...] = kvg
    kvg_pair[c] = kvg
    kvg_copy = pltpu.make_async_remote_copy(
        src_ref=kvg_pair.at[c],
        dst_ref=kvg_pair.at[c],
        send_sem=kvg_sem.at[0],
        recv_sem=kvg_sem.at[1],
        device_id={"head": sibling},
        device_id_type=MESH,
    )
    kvg_copy.start()
    for s in range(owners):

        @pl.when(c * owners + s != h)
        def _():
            pltpu.make_async_remote_copy(
                src_ref=wkv_out,
                dst_ref=wkv_half.at[pl.ds(s * rows, rows)],
                send_sem=wkv_send.at[s],
                recv_sem=wkv_recv.at[s],
                device_id={"head": sibling},
                device_id_type=MESH,
            ).wait_recv()

    pltpu.make_async_remote_copy(
        src_ref=kvg_pair.at[c],
        dst_ref=kvg_pair.at[1 - c],
        send_sem=kvg_sem.at[0],
        recv_sem=kvg_sem.at[1],
        device_id={"head": sibling},
        device_id_type=MESH,
    ).wait_recv()

    def z_copy(i, core, to_z, head):
        return pltpu.make_async_remote_copy(
            src_ref=z_out.at[i, core],
            dst_ref=z_in.at[z],
            send_sem=z_send.at[i, core],
            recv_sem=z_recv.at[z],
            device_id={"group": to_z, "head": head},
            device_id_type=MESH,
        )

    for i, core in chunks:
        b = lax.rem(z + 1 + i, per_half)
        to_z = c * per_half + b
        at = pl.multiple_of(b * wide, wide)
        acc = q_term(y, b, core)
        acc = acc + dot_nt(kvg_pair[core], wkv_half[pl.ds(at, wide), :])
        for k in range(1, chips):
            part_copies[k, i, core].wait_recv()
            acc = acc + part_in[k - 1, i, core].astype(F32)
        z_out[i, core] = acc.astype(BF16)
        away = jnp.logical_or(to_z != z, core != c)

        @pl.when(away)
        def _():
            z_copy(i, core, to_z, y * CORES + core).start()

        @pl.when(jnp.logical_not(away))
        def _():
            z_in[z] = z_out[i, core]

    source_core = z // per_half
    result = None
    for source in range(groups):

        @pl.when(jnp.logical_or(source != z, source_core != c))
        def _():
            pltpu.make_async_remote_copy(
                src_ref=z_out.at[0, 0],
                dst_ref=z_in.at[source],
                send_sem=z_send.at[0, 0],
                recv_sem=z_recv.at[source],
                device_id={"head": sibling},
                device_id_type=MESH,
            ).wait_recv()

        term = z_in[source].astype(F32)
        result = term if result is None else result + term
    out_ref[...] = result.astype(BF16)

    for j in range(owners):

        @pl.when(CORES * j + my_half != h)
        def _():
            wkv_copy(j).wait_send()

    for copy in [w_copy, dq_copy, kvg_copy, *dkv_copies, *part_copies.values()]:
        copy.wait_send()
    for i, core in chunks:
        to_z = c * per_half + lax.rem(z + 1 + i, per_half)

        @pl.when(jnp.logical_or(to_z != z, core != c))
        def _():
            z_copy(i, core, to_z, y * CORES + core).wait_send()


def shards(groups, heads, *args):
    query, kv, q_weight, kv_weight = args[0], args[2], args[6], args[8]
    seq, size = query.shape
    model = q_weight.shape[0]
    chips = heads // CORES
    tokens = seq // heads
    wide = model // groups
    half = model // CORES
    per_half = groups // CORES
    owners = heads // CORES
    dma = pltpu.SemaphoreType.DMA
    vmem = pl.BlockSpec(memory_space=pltpu.VMEM)
    return pl.pallas_call(
        functools.partial(kernel, groups, heads),
        out_shape=(
            jax.ShapeDtypeStruct((tokens, wide), BF16),
            jax.ShapeDtypeStruct((tokens, 2 * size), BF16),
        ),
        in_specs=[pl.BlockSpec(memory_space=pltpu.HBM)] * ARGS,
        out_specs=(vmem, vmem),
        scratch_shapes=[pltpu.VMEM(arg.shape, arg.dtype) for arg in args]
        + [
            dma((ARGS,)),
            pltpu.VMEM((half, 2 * size), BF16),
            pltpu.VMEM((half, size), BF16),
            pltpu.VMEM((half, 2 * size), BF16),
            pltpu.VMEM(kv_weight.shape, BF16),
            pltpu.VMEM((seq, 2 * size), BF16),
            pltpu.VMEM((seq, 2 * size), BF16),
            pltpu.VMEM((heads - 1, tokens, 2 * size), BF16),
            pltpu.VMEM((CORES, tokens, 2 * size), BF16),
            pltpu.VMEM((chips - 1, per_half, CORES, tokens, wide), BF16),
            pltpu.VMEM((chips - 1, per_half, CORES, tokens, wide), BF16),
            pltpu.VMEM((per_half, CORES, tokens, wide), BF16),
            pltpu.VMEM((groups, tokens, wide), BF16),
            pltpu.VMEM((seq, size), F32),
            pltpu.VMEM((seq, size), F32),
            dma((2,)),
            dma((owners,)),
            dma((owners,)),
            dma((2,)),
            dma((heads - 1,)),
            dma((heads - 1,)),
            dma((2,)),
            dma((chips - 1, per_half, CORES)),
            dma((chips - 1, per_half, CORES)),
            dma((per_half, CORES)),
            dma((groups,)),
        ],
        compiler_params=pltpu.CompilerParams(
            collective_id=0, has_side_effects=True, vmem_limit_bytes=63 * 1024 * 1024
        ),
    )(*args)


def solution(mesh):
    return jax.shard_map(
        functools.partial(shards, mesh.shape["group"], mesh.shape["head"]),
        mesh=mesh,
        in_specs=(
            P("dp", ("group", "head")),
            P(("group", "head"), "dp"),
            P("dp", "group"),
            P("group", "dp"),
            P("dp", ("group", "head")),
            P(("group", "head"), "dp"),
            P("dp", ("group", "head")),
            P("dp", ("group", "head")),
            P(("dp", "head"), "group"),
            P(("dp", "head"), "group"),
        ),
        out_specs=(P(("dp", "head"), "group"), P(("dp", "head"), "group")),
        check_vma=False,
    )
```

```python
import functools

import jax
import jax.numpy as jnp
from jax import lax
from jax.experimental import pallas as pl
from jax.experimental.pallas import tpu as pltpu
from jax.sharding import PartitionSpec as P

MESH = pl.DeviceIdType.MESH
F32 = jnp.float32
BF16 = jnp.bfloat16
CORES = 2
BLOCK = 32
ARGS = 10
PIECES = 2
LOAD_ORDER = (8, 9, 6, 7, 0, 1, 2, 3, 4, 5)


def power_of_two(exponent):
    scale = jnp.where(exponent == 0, 1.0, 0.0)
    for level in (-4, -3, -2, -1, 1, 2, 3, 4):
        scale = jnp.where(exponent == level, 2.0**level, scale)
    return scale.astype(F32)


def dequant_rows(mantissa, exponent):
    blocks, rows = exponent.shape
    scale = jnp.broadcast_to(power_of_two(exponent)[:, None, :], (blocks, BLOCK, rows))
    scale = scale.reshape(blocks * BLOCK, rows).T
    return (mantissa.astype(F32) * scale).astype(BF16)


def dequant_cols(mantissa, exponent):
    blocks, columns = exponent.shape
    scale = jnp.broadcast_to(power_of_two(exponent)[:, None, :], (blocks, BLOCK, columns))
    return (mantissa.astype(F32) * scale.reshape(blocks * BLOCK, columns)).astype(BF16)


def dot_nt(a, b):
    return lax.dot_general(a, b, (((1,), (1,)), ((), ())), preferred_element_type=F32)


def dot_tn(a, b):
    return lax.dot_general(a, b, (((0,), (0,)), ((), ())), preferred_element_type=F32)


def kernel(
    groups,
    heads,
    *refs,
):
    sources, (out_ref, kvg_ref) = refs[:ARGS], refs[ARGS : ARGS + 2]
    held = refs[ARGS + 2 : 2 * ARGS + 2]
    q_ref, qe_ref, kv_ref, kve_ref, do_ref, doe_ref, wq_ref, wqe_ref, wkv_ref, wkve_ref = held
    (
        load_sem,
        wq_pair,
        wq_out,
        wkv_half,
        wkv_out,
        dq_pair,
        dkv_out,
        dkv_near,
        dkv_sum,
        dkv_in,
        kvg_pair,
        part_out,
        part_in,
        z_out,
        z_in,
        dk_acc,
        dv_acc,
        w_sem,
        wkv_send,
        wkv_recv,
        dq_sem,
        near_send,
        near_recv,
        dkv_send,
        dkv_recv,
        kvg_sem,
        part_send,
        part_recv,
        z_send,
        z_recv,
    ) = refs[2 * ARGS + 2 :]
    seq, size = q_ref.shape
    model = wq_ref.shape[0]
    chips = heads // CORES
    tokens = seq // heads
    wide = model // groups
    half = model // CORES
    per_half = groups // CORES
    piece = tokens // PIECES
    rows = wkv_ref.shape[0]
    owners = heads // CORES
    scale = 1.0 / size**0.5

    z = lax.axis_index("group")
    h = lax.axis_index("head")
    y = h // CORES
    c = lax.rem(h, CORES)
    sibling = y * CORES + (1 - c)

    loads = [
        pltpu.make_async_copy(source, held[at], load_sem.at[at])
        for at, source in enumerate(sources)
    ]
    for at in LOAD_ORDER:
        loads[at].start()

    barrier = pltpu.get_barrier_semaphore()
    for k in range(1, heads):
        pl.semaphore_signal(
            barrier, inc=1, device_id={"head": lax.rem(h + k, heads)}, device_id_type=MESH
        )
    for k in range(1, groups):
        for core in range(CORES):
            pl.semaphore_signal(
                barrier,
                inc=1,
                device_id={"group": lax.rem(z + k, groups), "head": y * CORES + core},
                device_id_type=MESH,
            )

    def weight_rows(which):
        first = pl.multiple_of(which * half, half)
        first_e = pl.multiple_of(which * (half // BLOCK), half // BLOCK)
        return dequant_cols(
            wq_ref[pl.ds(first, half), :], wqe_ref[pl.ds(first_e, half // BLOCK), :]
        )

    for at in LOAD_ORDER[:2]:
        loads[at].wait()
    wkv_out[...] = dequant_cols(wkv_ref[...], wkve_ref[...])
    pl.semaphore_wait(barrier, heads - 1 + CORES * (groups - 1))

    my_half = h // owners
    my_slot = pl.multiple_of(lax.rem(h, owners) * rows, rows)

    def wkv_copy(j):
        return pltpu.make_async_remote_copy(
            src_ref=wkv_out,
            dst_ref=wkv_half.at[pl.ds(my_slot, rows)],
            send_sem=wkv_send.at[j],
            recv_sem=wkv_recv.at[lax.rem(h, owners)],
            device_id={"head": CORES * j + my_half},
            device_id_type=MESH,
        )

    for j in range(owners):

        @pl.when(CORES * j + my_half != h)
        def _():
            wkv_copy(j).start()

    for at in LOAD_ORDER[2:4]:
        loads[at].wait()
    wq_out[...] = weight_rows(1 - c)
    w_copy = pltpu.make_async_remote_copy(
        src_ref=wq_out,
        dst_ref=wq_pair.at[:, size:],
        send_sem=w_sem.at[0],
        recv_sem=w_sem.at[1],
        device_id={"head": sibling},
        device_id_type=MESH,
    )
    w_copy.start()
    wq_pair[:, :size] = weight_rows(c)

    @pl.when(my_half == c)
    def _():
        wkv_half[pl.ds(my_slot, rows), :] = wkv_out[...]

    for at in LOAD_ORDER[4:]:
        loads[at].wait()
    query = dequant_rows(q_ref[...], qe_ref[...])
    kv = dequant_rows(kv_ref[...], kve_ref[...])
    grad = dequant_rows(do_ref[...], doe_ref[...])
    keys, values = kv[:, :size], kv[:, size:]
    block = min(256, seq)
    for index in reversed(range(seq // block)):
        first, upper = index * block, (index + 1) * block
        q_block, do_block = query[first:upper], grad[first:upper]
        scores = dot_nt(keys[:upper], q_block)
        key_at = lax.broadcasted_iota(jnp.int32, (upper, block), 0)
        query_at = first + lax.broadcasted_iota(jnp.int32, (upper, block), 1)
        scores = jnp.where(key_at <= query_at, scores, -jnp.inf)
        expd = jnp.exp((scores - jnp.max(scores, axis=0, keepdims=True)) * scale)
        probs = expd * (1.0 / jnp.sum(expd, axis=0, keepdims=True))
        probs_b = probs.astype(BF16)
        dprob = dot_nt(values[:upper], do_block)
        delta = jnp.sum(probs_b.astype(F32) * dprob, axis=0, keepdims=True)
        dscore = (probs * (dprob - delta) * scale).astype(BF16)
        dq_pair[first:upper, :size] = dot_tn(dscore, keys[:upper]).astype(BF16)
        dk = jnp.dot(dscore, q_block, preferred_element_type=F32)
        dv = jnp.dot(probs_b, do_block, preferred_element_type=F32)
        if upper == seq:
            dk_acc[...] = dk
            dv_acc[...] = dv
        else:
            dk_acc[:upper, :] += dk
            dv_acc[:upper, :] += dv

    dq_copy = pltpu.make_async_remote_copy(
        src_ref=dq_pair.at[:, :size],
        dst_ref=dq_pair.at[:, size:],
        send_sem=dq_sem.at[0],
        recv_sem=dq_sem.at[1],
        device_id={"head": sibling},
        device_id_type=MESH,
    )
    dq_copy.start()
    dkv_out[:, :size] = dk_acc[...].astype(BF16)
    dkv_out[:, size:] = dv_acc[...].astype(BF16)

    def chip_rows(chip, core):
        return pl.ds(pl.multiple_of((chip * CORES + core) * tokens, tokens), tokens)

    near_copies = []
    for k in [*range(1, chips), 0]:
        copy = pltpu.make_async_remote_copy(
            src_ref=dkv_out.at[chip_rows(lax.rem(y + k, chips), 1 - c)],
            dst_ref=dkv_near.at[k],
            send_sem=near_send.at[k],
            recv_sem=near_recv.at[k],
            device_id={"head": sibling},
            device_id_type=MESH,
        )
        copy.start()
        near_copies.append(copy)
    dkv_copies = []
    for k in range(1, chips):
        to = lax.rem(y + k, chips)
        near_copies[k - 1].wait_recv()
        both = dkv_out[chip_rows(to, c), :].astype(F32) + dkv_near[k].astype(F32)
        dkv_sum[k - 1] = both.astype(BF16)
        copy = pltpu.make_async_remote_copy(
            src_ref=dkv_sum.at[k - 1],
            dst_ref=dkv_in.at[k - 1],
            send_sem=dkv_send.at[k - 1],
            recv_sem=dkv_recv.at[k - 1],
            device_id={"head": to * CORES + c},
            device_id_type=MESH,
        )
        copy.start()
        dkv_copies.append(copy)

    def q_term(chip, b, e):
        first = pl.multiple_of(chip * CORES * tokens + e * piece, piece)
        at = pl.multiple_of(b * wide, wide)
        return dot_nt(dq_pair[pl.ds(first, piece), :], wq_pair[pl.ds(at, wide), :])

    w_copy.wait_recv()
    dq_copy.wait_recv()
    chunks = [
        (i, core * PIECES + p)
        for i in range(per_half)
        for p in range(PIECES)
        for core in range(CORES)
    ]
    part_copies = {}
    for i, e in chunks:
        b = lax.rem(z + 1 + i, per_half)
        for k in range(1, chips):
            to = lax.rem(y + k, chips)
            part_out[k - 1, i, e] = q_term(to, b, e).astype(BF16)
            copy = pltpu.make_async_remote_copy(
                src_ref=part_out.at[k - 1, i, e],
                dst_ref=part_in.at[k - 1, i, e],
                send_sem=part_send.at[k - 1, i, e],
                recv_sem=part_recv.at[k - 1, i, e],
                device_id={"head": to * CORES + c},
                device_id_type=MESH,
            )
            copy.start()
            part_copies[k, i, e] = copy

    near_copies[-1].wait_recv()
    total = dkv_out[chip_rows(y, c), :].astype(F32) + dkv_near[0].astype(F32)
    for k in range(1, chips):
        dkv_copies[k - 1].wait_recv()
        total = total + dkv_in[k - 1].astype(F32)
    kvg = total.astype(BF16)
    kvg_ref[...] = kvg
    kvg_pair[c] = kvg
    kvg_copy = pltpu.make_async_remote_copy(
        src_ref=kvg_pair.at[c],
        dst_ref=kvg_pair.at[c],
        send_sem=kvg_sem.at[0],
        recv_sem=kvg_sem.at[1],
        device_id={"head": sibling},
        device_id_type=MESH,
    )
    kvg_copy.start()
    for s in range(owners):

        @pl.when(c * owners + s != h)
        def _():
            pltpu.make_async_remote_copy(
                src_ref=wkv_out,
                dst_ref=wkv_half.at[pl.ds(s * rows, rows)],
                send_sem=wkv_send.at[s],
                recv_sem=wkv_recv.at[s],
                device_id={"head": sibling},
                device_id_type=MESH,
            ).wait_recv()

    pltpu.make_async_remote_copy(
        src_ref=kvg_pair.at[c],
        dst_ref=kvg_pair.at[1 - c],
        send_sem=kvg_sem.at[0],
        recv_sem=kvg_sem.at[1],
        device_id={"head": sibling},
        device_id_type=MESH,
    ).wait_recv()

    def z_copy(i, e, to_z):
        return pltpu.make_async_remote_copy(
            src_ref=z_out.at[i, e],
            dst_ref=z_in.at[z, e % PIECES],
            send_sem=z_send.at[i, e],
            recv_sem=z_recv.at[z, e % PIECES],
            device_id={"group": to_z, "head": y * CORES + e // PIECES},
            device_id_type=MESH,
        )

    for i, e in chunks:
        b = lax.rem(z + 1 + i, per_half)
        to_z = c * per_half + b
        at = pl.multiple_of(b * wide, wide)
        acc = q_term(y, b, e)
        kvg_piece = kvg_pair[e // PIECES, pl.ds(e % PIECES * piece, piece), :]
        acc = acc + dot_nt(kvg_piece, wkv_half[pl.ds(at, wide), :])
        for k in range(1, chips):
            part_copies[k, i, e].wait_recv()
            acc = acc + part_in[k - 1, i, e].astype(F32)
        z_out[i, e] = acc.astype(BF16)
        away = jnp.logical_or(to_z != z, e // PIECES != c)

        @pl.when(away)
        def _():
            z_copy(i, e, to_z).start()

        @pl.when(jnp.logical_not(away))
        def _():
            z_in[z, e % PIECES] = z_out[i, e]

    source_core = z // per_half
    for p in range(PIECES):
        result = None
        for source in range(groups):

            @pl.when(jnp.logical_or(source != z, source_core != c))
            def _():
                pltpu.make_async_remote_copy(
                    src_ref=z_out.at[0, 0],
                    dst_ref=z_in.at[source, p],
                    send_sem=z_send.at[0, 0],
                    recv_sem=z_recv.at[source, p],
                    device_id={"head": sibling},
                    device_id_type=MESH,
                ).wait_recv()

            term = z_in[source, p].astype(F32)
            result = term if result is None else result + term
        out_ref[p * piece : (p + 1) * piece, :] = result.astype(BF16)

    for j in range(owners):

        @pl.when(CORES * j + my_half != h)
        def _():
            wkv_copy(j).wait_send()

    for copy in [w_copy, dq_copy, kvg_copy, *near_copies, *dkv_copies, *part_copies.values()]:
        copy.wait_send()
    for i, e in chunks:
        to_z = c * per_half + lax.rem(z + 1 + i, per_half)

        @pl.when(jnp.logical_or(to_z != z, e // PIECES != c))
        def _():
            z_copy(i, e, to_z).wait_send()


def shards(groups, heads, *args):
    query, kv, q_weight, kv_weight = args[0], args[2], args[6], args[8]
    seq, size = query.shape
    model = q_weight.shape[0]
    chips = heads // CORES
    tokens = seq // heads
    piece = tokens // PIECES
    wide = model // groups
    half = model // CORES
    per_half = groups // CORES
    owners = heads // CORES
    dma = pltpu.SemaphoreType.DMA
    vmem = pl.BlockSpec(memory_space=pltpu.VMEM)
    return pl.pallas_call(
        functools.partial(kernel, groups, heads),
        out_shape=(
            jax.ShapeDtypeStruct((tokens, wide), BF16),
            jax.ShapeDtypeStruct((tokens, 2 * size), BF16),
        ),
        in_specs=[pl.BlockSpec(memory_space=pltpu.HBM)] * ARGS,
        out_specs=(vmem, vmem),
        scratch_shapes=[pltpu.VMEM(arg.shape, arg.dtype) for arg in args]
        + [
            dma((ARGS,)),
            pltpu.VMEM((half, 2 * size), BF16),
            pltpu.VMEM((half, size), BF16),
            pltpu.VMEM((half, 2 * size), BF16),
            pltpu.VMEM(kv_weight.shape, BF16),
            pltpu.VMEM((seq, 2 * size), BF16),
            pltpu.VMEM((seq, 2 * size), BF16),
            pltpu.VMEM((chips, tokens, 2 * size), BF16),
            pltpu.VMEM((chips - 1, tokens, 2 * size), BF16),
            pltpu.VMEM((chips - 1, tokens, 2 * size), BF16),
            pltpu.VMEM((CORES, tokens, 2 * size), BF16),
            pltpu.VMEM((chips - 1, per_half, CORES * PIECES, piece, wide), BF16),
            pltpu.VMEM((chips - 1, per_half, CORES * PIECES, piece, wide), BF16),
            pltpu.VMEM((per_half, CORES * PIECES, piece, wide), BF16),
            pltpu.VMEM((groups, PIECES, piece, wide), BF16),
            pltpu.VMEM((seq, size), F32),
            pltpu.VMEM((seq, size), F32),
            dma((2,)),
            dma((owners,)),
            dma((owners,)),
            dma((2,)),
            dma((chips,)),
            dma((chips,)),
            dma((chips - 1,)),
            dma((chips - 1,)),
            dma((2,)),
            dma((chips - 1, per_half, CORES * PIECES)),
            dma((chips - 1, per_half, CORES * PIECES)),
            dma((per_half, CORES * PIECES)),
            dma((groups, PIECES)),
        ],
        compiler_params=pltpu.CompilerParams(
            collective_id=0, has_side_effects=True, vmem_limit_bytes=63 * 1024 * 1024
        ),
    )(*args)


def solution(mesh):
    return jax.shard_map(
        functools.partial(shards, mesh.shape["group"], mesh.shape["head"]),
        mesh=mesh,
        in_specs=(
            P("dp", ("group", "head")),
            P(("group", "head"), "dp"),
            P("dp", "group"),
            P("group", "dp"),
            P("dp", ("group", "head")),
            P(("group", "head"), "dp"),
            P("dp", ("group", "head")),
            P("dp", ("group", "head")),
            P(("dp", "head"), "group"),
            P(("dp", "head"), "group"),
        ),
        out_specs=(P(("dp", "head"), "group"), P(("dp", "head"), "group")),
        check_vma=False,
    )
```

```python
import functools

import jax
import jax.numpy as jnp
from jax import lax
from jax.experimental import pallas as pl
from jax.experimental.pallas import tpu as pltpu
from jax.sharding import PartitionSpec as P

MESH = pl.DeviceIdType.MESH
F32 = jnp.float32
BF16 = jnp.bfloat16
CORES = 2
BLOCK = 32
ARGS = 10
PIECES = 2
AHEAD = 4
LOAD_ORDER = (8, 9, 6, 7, 0, 1, 2, 3, 4, 5)


def power_of_two(exponent):
    scale = jnp.where(exponent == 0, 1.0, 0.0)
    for level in (-4, -3, -2, -1, 1, 2, 3, 4):
        scale = jnp.where(exponent == level, 2.0**level, scale)
    return scale.astype(F32)


def dequant_rows(mantissa, exponent):
    blocks, rows = exponent.shape
    scale = jnp.broadcast_to(power_of_two(exponent)[:, None, :], (blocks, BLOCK, rows))
    scale = scale.reshape(blocks * BLOCK, rows).T
    return (mantissa.astype(F32) * scale).astype(BF16)


def dequant_cols(mantissa, exponent):
    blocks, columns = exponent.shape
    scale = jnp.broadcast_to(power_of_two(exponent)[:, None, :], (blocks, BLOCK, columns))
    return (mantissa.astype(F32) * scale.reshape(blocks * BLOCK, columns)).astype(BF16)


def dot_nt(a, b):
    return lax.dot_general(a, b, (((1,), (1,)), ((), ())), preferred_element_type=F32)


def dot_tn(a, b):
    return lax.dot_general(a, b, (((0,), (0,)), ((), ())), preferred_element_type=F32)


def kernel(
    groups,
    heads,
    *refs,
):
    sources, (out_ref, kvg_ref) = refs[:ARGS], refs[ARGS : ARGS + 2]
    held = refs[ARGS + 2 : 2 * ARGS + 2]
    q_ref, qe_ref, kv_ref, kve_ref, do_ref, doe_ref, wq_ref, wqe_ref, wkv_ref, wkve_ref = held
    (
        load_sem,
        wq_pair,
        wq_out,
        wkv_half,
        wkv_out,
        dq_pair,
        dkv_out,
        dkv_near,
        dkv_sum,
        dkv_in,
        kvg_pair,
        part_out,
        part_in,
        z_out,
        z_in,
        dk_acc,
        dv_acc,
        w_sem,
        wkv_send,
        wkv_recv,
        dq_sem,
        near_send,
        near_recv,
        dkv_send,
        dkv_recv,
        kvg_sem,
        part_send,
        part_recv,
        z_send,
        z_recv,
    ) = refs[2 * ARGS + 2 :]
    seq, size = q_ref.shape
    model = wq_ref.shape[0]
    chips = heads // CORES
    tokens = seq // heads
    wide = model // groups
    half = model // CORES
    per_half = groups // CORES
    piece = tokens // PIECES
    rows = wkv_ref.shape[0]
    owners = heads // CORES
    scale = 1.0 / size**0.5

    z = lax.axis_index("group")
    h = lax.axis_index("head")
    y = h // CORES
    c = lax.rem(h, CORES)
    sibling = y * CORES + (1 - c)

    loads = [
        pltpu.make_async_copy(source, held[at], load_sem.at[at])
        for at, source in enumerate(sources)
    ]
    for at in LOAD_ORDER:
        loads[at].start()

    barrier = pltpu.get_barrier_semaphore()
    for k in range(1, heads):
        pl.semaphore_signal(
            barrier, inc=1, device_id={"head": lax.rem(h + k, heads)}, device_id_type=MESH
        )
    for k in range(1, groups):
        for core in range(CORES):
            pl.semaphore_signal(
                barrier,
                inc=1,
                device_id={"group": lax.rem(z + k, groups), "head": y * CORES + core},
                device_id_type=MESH,
            )

    def weight_rows(which):
        first = pl.multiple_of(which * half, half)
        first_e = pl.multiple_of(which * (half // BLOCK), half // BLOCK)
        return dequant_cols(
            wq_ref[pl.ds(first, half), :], wqe_ref[pl.ds(first_e, half // BLOCK), :]
        )

    for at in LOAD_ORDER[:2]:
        loads[at].wait()
    wkv_out[...] = dequant_cols(wkv_ref[...], wkve_ref[...])
    pl.semaphore_wait(barrier, heads - 1 + CORES * (groups - 1))

    my_half = h // owners
    my_slot = pl.multiple_of(lax.rem(h, owners) * rows, rows)

    def wkv_copy(j):
        return pltpu.make_async_remote_copy(
            src_ref=wkv_out,
            dst_ref=wkv_half.at[pl.ds(my_slot, rows)],
            send_sem=wkv_send.at[j],
            recv_sem=wkv_recv.at[lax.rem(h, owners)],
            device_id={"head": CORES * j + my_half},
            device_id_type=MESH,
        )

    for j in range(owners):

        @pl.when(CORES * j + my_half != h)
        def _():
            wkv_copy(j).start()

    for at in LOAD_ORDER[2:4]:
        loads[at].wait()
    wq_out[...] = weight_rows(1 - c)
    w_copy = pltpu.make_async_remote_copy(
        src_ref=wq_out,
        dst_ref=wq_pair.at[:, size:],
        send_sem=w_sem.at[0],
        recv_sem=w_sem.at[1],
        device_id={"head": sibling},
        device_id_type=MESH,
    )
    w_copy.start()
    wq_pair[:, :size] = weight_rows(c)

    @pl.when(my_half == c)
    def _():
        wkv_half[pl.ds(my_slot, rows), :] = wkv_out[...]

    for at in LOAD_ORDER[4:]:
        loads[at].wait()
    query = dequant_rows(q_ref[...], qe_ref[...])
    kv = dequant_rows(kv_ref[...], kve_ref[...])
    grad = dequant_rows(do_ref[...], doe_ref[...])
    keys, values = kv[:, :size], kv[:, size:]
    block = min(256, seq)
    for index in reversed(range(seq // block)):
        first, upper = index * block, (index + 1) * block
        q_block, do_block = query[first:upper], grad[first:upper]
        scores = dot_nt(keys[:upper], q_block)
        key_at = lax.broadcasted_iota(jnp.int32, (upper, block), 0)
        query_at = first + lax.broadcasted_iota(jnp.int32, (upper, block), 1)
        scores = jnp.where(key_at <= query_at, scores, -jnp.inf)
        expd = jnp.exp((scores - jnp.max(scores, axis=0, keepdims=True)) * scale)
        probs = expd * (1.0 / jnp.sum(expd, axis=0, keepdims=True))
        probs_b = probs.astype(BF16)
        dprob = dot_nt(values[:upper], do_block)
        delta = jnp.sum(probs_b.astype(F32) * dprob, axis=0, keepdims=True)
        dscore = (probs * (dprob - delta) * scale).astype(BF16)
        dq_pair[first:upper, :size] = dot_tn(dscore, keys[:upper]).astype(BF16)
        dk = jnp.dot(dscore, q_block, preferred_element_type=F32)
        dv = jnp.dot(probs_b, do_block, preferred_element_type=F32)
        if upper == seq:
            dk_acc[...] = dk
            dv_acc[...] = dv
        else:
            dk_acc[:upper, :] += dk
            dv_acc[:upper, :] += dv

    dq_copy = pltpu.make_async_remote_copy(
        src_ref=dq_pair.at[:, :size],
        dst_ref=dq_pair.at[:, size:],
        send_sem=dq_sem.at[0],
        recv_sem=dq_sem.at[1],
        device_id={"head": sibling},
        device_id_type=MESH,
    )
    dq_copy.start()
    dkv_out[:, :size] = dk_acc[...].astype(BF16)
    dkv_out[:, size:] = dv_acc[...].astype(BF16)

    def chip_rows(chip, core):
        return pl.ds(pl.multiple_of((chip * CORES + core) * tokens, tokens), tokens)

    near_copies = []
    for k in [*range(1, chips), 0]:
        copy = pltpu.make_async_remote_copy(
            src_ref=dkv_out.at[chip_rows(lax.rem(y + k, chips), 1 - c)],
            dst_ref=dkv_near.at[k],
            send_sem=near_send.at[k],
            recv_sem=near_recv.at[k],
            device_id={"head": sibling},
            device_id_type=MESH,
        )
        copy.start()
        near_copies.append(copy)
    dkv_copies = []
    for k in range(1, chips):
        to = lax.rem(y + k, chips)
        near_copies[k - 1].wait_recv()
        both = dkv_out[chip_rows(to, c), :].astype(F32) + dkv_near[k].astype(F32)
        dkv_sum[k - 1] = both.astype(BF16)
        copy = pltpu.make_async_remote_copy(
            src_ref=dkv_sum.at[k - 1],
            dst_ref=dkv_in.at[k - 1],
            send_sem=dkv_send.at[k - 1],
            recv_sem=dkv_recv.at[k - 1],
            device_id={"head": to * CORES + c},
            device_id_type=MESH,
        )
        copy.start()
        dkv_copies.append(copy)

    def q_term(chip, b, e):
        first = pl.multiple_of(chip * CORES * tokens + e * piece, piece)
        at = pl.multiple_of(b * wide, wide)
        return dot_nt(dq_pair[pl.ds(first, piece), :], wq_pair[pl.ds(at, wide), :])

    w_copy.wait_recv()
    dq_copy.wait_recv()
    chunks = [
        (i, core * PIECES + p)
        for i in range(per_half)
        for p in range(PIECES)
        for core in range(CORES)
    ]
    part_copies = {}

    def send_part(i, e):
        b = lax.rem(z + 1 + i, per_half)
        for k in range(1, chips):
            to = lax.rem(y + k, chips)
            part_out[k - 1, i, e] = q_term(to, b, e).astype(BF16)
            copy = pltpu.make_async_remote_copy(
                src_ref=part_out.at[k - 1, i, e],
                dst_ref=part_in.at[k - 1, i, e],
                send_sem=part_send.at[k - 1, i, e],
                recv_sem=part_recv.at[k - 1, i, e],
                device_id={"head": to * CORES + c},
                device_id_type=MESH,
            )
            copy.start()
            part_copies[k, i, e] = copy

    for i, e in chunks[:AHEAD]:
        send_part(i, e)

    near_copies[-1].wait_recv()
    total = dkv_out[chip_rows(y, c), :].astype(F32) + dkv_near[0].astype(F32)
    for k in range(1, chips):
        dkv_copies[k - 1].wait_recv()
        total = total + dkv_in[k - 1].astype(F32)
    kvg = total.astype(BF16)
    kvg_ref[...] = kvg
    kvg_pair[c] = kvg
    kvg_copy = pltpu.make_async_remote_copy(
        src_ref=kvg_pair.at[c],
        dst_ref=kvg_pair.at[c],
        send_sem=kvg_sem.at[0],
        recv_sem=kvg_sem.at[1],
        device_id={"head": sibling},
        device_id_type=MESH,
    )
    kvg_copy.start()
    for s in range(owners):

        @pl.when(c * owners + s != h)
        def _():
            pltpu.make_async_remote_copy(
                src_ref=wkv_out,
                dst_ref=wkv_half.at[pl.ds(s * rows, rows)],
                send_sem=wkv_send.at[s],
                recv_sem=wkv_recv.at[s],
                device_id={"head": sibling},
                device_id_type=MESH,
            ).wait_recv()

    pltpu.make_async_remote_copy(
        src_ref=kvg_pair.at[c],
        dst_ref=kvg_pair.at[1 - c],
        send_sem=kvg_sem.at[0],
        recv_sem=kvg_sem.at[1],
        device_id={"head": sibling},
        device_id_type=MESH,
    ).wait_recv()

    def z_copy(i, e, to_z):
        return pltpu.make_async_remote_copy(
            src_ref=z_out.at[i, e],
            dst_ref=z_in.at[z, e % PIECES],
            send_sem=z_send.at[i, e],
            recv_sem=z_recv.at[z, e % PIECES],
            device_id={"group": to_z, "head": y * CORES + e // PIECES},
            device_id_type=MESH,
        )

    for n, (i, e) in enumerate(chunks):
        b = lax.rem(z + 1 + i, per_half)
        to_z = c * per_half + b
        at = pl.multiple_of(b * wide, wide)
        acc = q_term(y, b, e)
        kvg_piece = kvg_pair[e // PIECES, pl.ds(e % PIECES * piece, piece), :]
        acc = acc + dot_nt(kvg_piece, wkv_half[pl.ds(at, wide), :])
        for k in range(1, chips):
            part_copies[k, i, e].wait_recv()
            acc = acc + part_in[k - 1, i, e].astype(F32)
        z_out[i, e] = acc.astype(BF16)
        away = jnp.logical_or(to_z != z, e // PIECES != c)

        @pl.when(away)
        def _():
            z_copy(i, e, to_z).start()

        @pl.when(jnp.logical_not(away))
        def _():
            z_in[z, e % PIECES] = z_out[i, e]

        if n + AHEAD < len(chunks):
            for k in range(1, chips):
                part_copies[k, i, e].wait_send()
            send_part(*chunks[n + AHEAD])

    source_core = z // per_half
    for p in range(PIECES):
        result = None
        for source in range(groups):

            @pl.when(jnp.logical_or(source != z, source_core != c))
            def _():
                pltpu.make_async_remote_copy(
                    src_ref=z_out.at[0, 0],
                    dst_ref=z_in.at[source, p],
                    send_sem=z_send.at[0, 0],
                    recv_sem=z_recv.at[source, p],
                    device_id={"head": sibling},
                    device_id_type=MESH,
                ).wait_recv()

            term = z_in[source, p].astype(F32)
            result = term if result is None else result + term
        out_ref[p * piece : (p + 1) * piece, :] = result.astype(BF16)

    for j in range(owners):

        @pl.when(CORES * j + my_half != h)
        def _():
            wkv_copy(j).wait_send()

    for copy in [w_copy, dq_copy, kvg_copy, *near_copies, *dkv_copies]:
        copy.wait_send()
    for i, e in chunks[-AHEAD:]:
        for k in range(1, chips):
            part_copies[k, i, e].wait_send()
    for i, e in chunks:
        to_z = c * per_half + lax.rem(z + 1 + i, per_half)

        @pl.when(jnp.logical_or(to_z != z, e // PIECES != c))
        def _():
            z_copy(i, e, to_z).wait_send()


def shards(groups, heads, *args):
    query, kv, q_weight, kv_weight = args[0], args[2], args[6], args[8]
    seq, size = query.shape
    model = q_weight.shape[0]
    chips = heads // CORES
    tokens = seq // heads
    piece = tokens // PIECES
    wide = model // groups
    half = model // CORES
    per_half = groups // CORES
    owners = heads // CORES
    dma = pltpu.SemaphoreType.DMA
    vmem = pl.BlockSpec(memory_space=pltpu.VMEM)
    return pl.pallas_call(
        functools.partial(kernel, groups, heads),
        out_shape=(
            pltpu.VMEM((tokens, wide), BF16),
            pltpu.VMEM((tokens, 2 * size), BF16),
        ),
        in_specs=[pl.BlockSpec(memory_space=pltpu.HBM)] * ARGS,
        out_specs=(vmem, vmem),
        scratch_shapes=[pltpu.VMEM(arg.shape, arg.dtype) for arg in args]
        + [
            dma((ARGS,)),
            pltpu.VMEM((half, 2 * size), BF16),
            pltpu.VMEM((half, size), BF16),
            pltpu.VMEM((half, 2 * size), BF16),
            pltpu.VMEM(kv_weight.shape, BF16),
            pltpu.VMEM((seq, 2 * size), BF16),
            pltpu.VMEM((seq, 2 * size), BF16),
            pltpu.VMEM((chips, tokens, 2 * size), BF16),
            pltpu.VMEM((chips - 1, tokens, 2 * size), BF16),
            pltpu.VMEM((chips - 1, tokens, 2 * size), BF16),
            pltpu.VMEM((CORES, tokens, 2 * size), BF16),
            pltpu.VMEM((chips - 1, per_half, CORES * PIECES, piece, wide), BF16),
            pltpu.VMEM((chips - 1, per_half, CORES * PIECES, piece, wide), BF16),
            pltpu.VMEM((per_half, CORES * PIECES, piece, wide), BF16),
            pltpu.VMEM((groups, PIECES, piece, wide), BF16),
            pltpu.VMEM((seq, size), F32),
            pltpu.VMEM((seq, size), F32),
            dma((2,)),
            dma((owners,)),
            dma((owners,)),
            dma((2,)),
            dma((chips,)),
            dma((chips,)),
            dma((chips - 1,)),
            dma((chips - 1,)),
            dma((2,)),
            dma((chips - 1, per_half, CORES * PIECES)),
            dma((chips - 1, per_half, CORES * PIECES)),
            dma((per_half, CORES * PIECES)),
            dma((groups, PIECES)),
        ],
        compiler_params=pltpu.CompilerParams(
            collective_id=0, has_side_effects=True, vmem_limit_bytes=55 * 1024 * 1024
        ),
    )(*args)


def solution(mesh):
    return jax.shard_map(
        functools.partial(shards, mesh.shape["group"], mesh.shape["head"]),
        mesh=mesh,
        in_specs=(
            P("dp", ("group", "head")),
            P(("group", "head"), "dp"),
            P("dp", "group"),
            P("group", "dp"),
            P("dp", ("group", "head")),
            P(("group", "head"), "dp"),
            P("dp", ("group", "head")),
            P("dp", ("group", "head")),
            P(("dp", "head"), "group"),
            P(("dp", "head"), "group"),
        ),
        out_specs=(P(("dp", "head"), "group"), P(("dp", "head"), "group")),
        check_vma=False,
    )
```

```python
import functools

import jax
import jax.numpy as jnp
from jax import lax
from jax.experimental import pallas as pl
from jax.experimental.pallas import tpu as pltpu
from jax.sharding import PartitionSpec as P

MESH = pl.DeviceIdType.MESH
F32 = jnp.float32
BF16 = jnp.bfloat16
CORES = 2
BLOCK = 32
ARGS = 10
PIECES = 2
AHEAD = 4
LOAD_ORDER = (8, 9, 6, 7, 0, 1, 2, 3, 4, 5)


def power_of_two(exponent):
    scale = jnp.where(exponent == 0, 1.0, 0.0)
    for level in (-4, -3, -2, -1, 1, 2, 3, 4):
        scale = jnp.where(exponent == level, 2.0**level, scale)
    return scale.astype(F32)


def dequant_rows(mantissa, exponent):
    blocks, rows = exponent.shape
    scale = jnp.broadcast_to(power_of_two(exponent)[:, None, :], (blocks, BLOCK, rows))
    scale = scale.reshape(blocks * BLOCK, rows).T
    return (mantissa.astype(F32) * scale).astype(BF16)


def dequant_cols(mantissa, exponent):
    blocks, columns = exponent.shape
    scale = jnp.broadcast_to(power_of_two(exponent)[:, None, :], (blocks, BLOCK, columns))
    return (mantissa.astype(F32) * scale.reshape(blocks * BLOCK, columns)).astype(BF16)


def dot_nt(a, b):
    return lax.dot_general(a, b, (((1,), (1,)), ((), ())), preferred_element_type=F32)


def dot_tn(a, b):
    return lax.dot_general(a, b, (((0,), (0,)), ((), ())), preferred_element_type=F32)


def kernel(
    groups,
    heads,
    *refs,
):
    sources, (out_ref, kvg_ref) = refs[:ARGS], refs[ARGS : ARGS + 2]
    held = refs[ARGS + 2 : 2 * ARGS + 2]
    q_ref, qe_ref, kv_ref, kve_ref, do_ref, doe_ref, wq_ref, wqe_ref, wkv_ref, wkve_ref = held
    (
        load_sem,
        wq_pair,
        wq_out,
        wkv_half,
        wkv_out,
        dq_pair,
        dkv_out,
        dkv_near,
        dkv_sum,
        dkv_in,
        kvg_pair,
        part_out,
        part_in,
        z_out,
        z_in,
        dk_acc,
        dv_acc,
        w_sem,
        wkv_send,
        wkv_recv,
        dq_send,
        dq_recv,
        near_send,
        near_recv,
        dkv_send,
        dkv_recv,
        kvg_sem,
        part_send,
        part_recv,
        z_send,
        z_recv,
    ) = refs[2 * ARGS + 2 :]
    seq, size = q_ref.shape
    model = wq_ref.shape[0]
    chips = heads // CORES
    tokens = seq // heads
    wide = model // groups
    half = model // CORES
    per_half = groups // CORES
    piece = tokens // PIECES
    rows = wkv_ref.shape[0]
    owners = heads // CORES
    scale = 1.0 / size**0.5

    z = lax.axis_index("group")
    h = lax.axis_index("head")
    y = h // CORES
    c = lax.rem(h, CORES)
    sibling = y * CORES + (1 - c)

    loads = [
        pltpu.make_async_copy(source, held[at], load_sem.at[at])
        for at, source in enumerate(sources)
    ]
    for at in LOAD_ORDER:
        loads[at].start()

    barrier = pltpu.get_barrier_semaphore()
    for k in range(1, heads):
        pl.semaphore_signal(
            barrier, inc=1, device_id={"head": lax.rem(h + k, heads)}, device_id_type=MESH
        )
    for k in range(1, groups):
        for core in range(CORES):
            pl.semaphore_signal(
                barrier,
                inc=1,
                device_id={"group": lax.rem(z + k, groups), "head": y * CORES + core},
                device_id_type=MESH,
            )

    def weight_rows(which):
        first = pl.multiple_of(which * half, half)
        first_e = pl.multiple_of(which * (half // BLOCK), half // BLOCK)
        return dequant_cols(
            wq_ref[pl.ds(first, half), :], wqe_ref[pl.ds(first_e, half // BLOCK), :]
        )

    for at in LOAD_ORDER[:2]:
        loads[at].wait()
    wkv_out[...] = dequant_cols(wkv_ref[...], wkve_ref[...])
    pl.semaphore_wait(barrier, heads - 1 + CORES * (groups - 1))

    my_half = h // owners
    my_slot = pl.multiple_of(lax.rem(h, owners) * rows, rows)

    def wkv_copy(j):
        return pltpu.make_async_remote_copy(
            src_ref=wkv_out,
            dst_ref=wkv_half.at[pl.ds(my_slot, rows)],
            send_sem=wkv_send.at[j],
            recv_sem=wkv_recv.at[lax.rem(h, owners)],
            device_id={"head": CORES * j + my_half},
            device_id_type=MESH,
        )

    for j in range(owners):

        @pl.when(CORES * j + my_half != h)
        def _():
            wkv_copy(j).start()

    for at in LOAD_ORDER[2:4]:
        loads[at].wait()
    wq_out[...] = weight_rows(1 - c)
    w_copy = pltpu.make_async_remote_copy(
        src_ref=wq_out,
        dst_ref=wq_pair.at[:, size:],
        send_sem=w_sem.at[0],
        recv_sem=w_sem.at[1],
        device_id={"head": sibling},
        device_id_type=MESH,
    )
    w_copy.start()
    wq_pair[:, :size] = weight_rows(c)

    @pl.when(my_half == c)
    def _():
        wkv_half[pl.ds(my_slot, rows), :] = wkv_out[...]

    for at in LOAD_ORDER[4:]:
        loads[at].wait()
    kv = dequant_rows(kv_ref[...], kve_ref[...])
    keys, values = kv[:, :size], kv[:, size:]
    block = CORES * tokens
    key_at = lax.broadcasted_iota(jnp.int32, (seq, block), 0)
    query_at = lax.broadcasted_iota(jnp.int32, (seq, block), 1)
    dq_copies = []
    for k in [*range(1, chips), 0]:
        first = pl.multiple_of(lax.rem(y + k, chips) * block, block)
        at = pl.ds(first, block)
        q_block = dequant_rows(q_ref[at, :], qe_ref[:, at])
        do_block = dequant_rows(do_ref[at, :], doe_ref[:, at])
        scores = dot_nt(keys, q_block)
        scores = jnp.where(key_at <= first + query_at, scores, -jnp.inf)
        expd = jnp.exp((scores - jnp.max(scores, axis=0, keepdims=True)) * scale)
        probs = expd * (1.0 / jnp.sum(expd, axis=0, keepdims=True))
        probs_b = probs.astype(BF16)
        dprob = dot_nt(values, do_block)
        delta = jnp.sum(probs_b.astype(F32) * dprob, axis=0, keepdims=True)
        dscore = (probs * (dprob - delta) * scale).astype(BF16)
        dq_pair[at, :size] = dot_tn(dscore, keys).astype(BF16)
        copy = pltpu.make_async_remote_copy(
            src_ref=dq_pair.at[at, pl.ds(0, size)],
            dst_ref=dq_pair.at[at, pl.ds(size, size)],
            send_sem=dq_send.at[k],
            recv_sem=dq_recv.at[k],
            device_id={"head": sibling},
            device_id_type=MESH,
        )
        copy.start()
        dq_copies.append(copy)
        dk = jnp.dot(dscore, q_block, preferred_element_type=F32)
        dv = jnp.dot(probs_b, do_block, preferred_element_type=F32)
        if len(dq_copies) == 1:
            dk_acc[...] = dk
            dv_acc[...] = dv
        else:
            dk_acc[...] += dk
            dv_acc[...] += dv

    dkv_out[:, :size] = dk_acc[...].astype(BF16)
    dkv_out[:, size:] = dv_acc[...].astype(BF16)

    def chip_rows(chip, core):
        return pl.ds(pl.multiple_of((chip * CORES + core) * tokens, tokens), tokens)

    near_copies = []
    for k in [*range(1, chips), 0]:
        copy = pltpu.make_async_remote_copy(
            src_ref=dkv_out.at[chip_rows(lax.rem(y + k, chips), 1 - c)],
            dst_ref=dkv_near.at[k],
            send_sem=near_send.at[k],
            recv_sem=near_recv.at[k],
            device_id={"head": sibling},
            device_id_type=MESH,
        )
        copy.start()
        near_copies.append(copy)
    def q_term(chip, b, e):
        first = pl.multiple_of(chip * CORES * tokens + e * piece, piece)
        at = pl.multiple_of(b * wide, wide)
        return dot_nt(dq_pair[pl.ds(first, piece), :], wq_pair[pl.ds(at, wide), :])

    w_copy.wait_recv()
    for copy in dq_copies[:-1]:
        copy.wait_recv()
    chunks = [
        (i, core * PIECES + p)
        for i in range(per_half)
        for p in range(PIECES)
        for core in range(CORES)
    ]
    part_copies = {}

    def send_part(i, e):
        b = lax.rem(z + 1 + i, per_half)
        for k in range(1, chips):
            to = lax.rem(y + k, chips)
            part_out[k - 1, i, e] = q_term(to, b, e).astype(BF16)
            copy = pltpu.make_async_remote_copy(
                src_ref=part_out.at[k - 1, i, e],
                dst_ref=part_in.at[k - 1, i, e],
                send_sem=part_send.at[k - 1, i, e],
                recv_sem=part_recv.at[k - 1, i, e],
                device_id={"head": to * CORES + c},
                device_id_type=MESH,
            )
            copy.start()
            part_copies[k, i, e] = copy

    for i, e in chunks[: AHEAD // 2]:
        send_part(i, e)

    dkv_copies = []
    for k in range(1, chips):
        to = lax.rem(y + k, chips)
        near_copies[k - 1].wait_recv()
        both = dkv_out[chip_rows(to, c), :].astype(F32) + dkv_near[k].astype(F32)
        dkv_sum[k - 1] = both.astype(BF16)
        copy = pltpu.make_async_remote_copy(
            src_ref=dkv_sum.at[k - 1],
            dst_ref=dkv_in.at[k - 1],
            send_sem=dkv_send.at[k - 1],
            recv_sem=dkv_recv.at[k - 1],
            device_id={"head": to * CORES + c},
            device_id_type=MESH,
        )
        copy.start()
        dkv_copies.append(copy)

    for i, e in chunks[AHEAD // 2 : AHEAD]:
        send_part(i, e)
    dq_copies[-1].wait_recv()

    near_copies[-1].wait_recv()
    total = dkv_out[chip_rows(y, c), :].astype(F32) + dkv_near[0].astype(F32)
    for k in range(1, chips):
        dkv_copies[k - 1].wait_recv()
        total = total + dkv_in[k - 1].astype(F32)
    kvg = total.astype(BF16)
    kvg_ref[...] = kvg
    kvg_pair[c] = kvg
    kvg_copy = pltpu.make_async_remote_copy(
        src_ref=kvg_pair.at[c],
        dst_ref=kvg_pair.at[c],
        send_sem=kvg_sem.at[0],
        recv_sem=kvg_sem.at[1],
        device_id={"head": sibling},
        device_id_type=MESH,
    )
    kvg_copy.start()
    for s in range(owners):

        @pl.when(c * owners + s != h)
        def _():
            pltpu.make_async_remote_copy(
                src_ref=wkv_out,
                dst_ref=wkv_half.at[pl.ds(s * rows, rows)],
                send_sem=wkv_send.at[s],
                recv_sem=wkv_recv.at[s],
                device_id={"head": sibling},
                device_id_type=MESH,
            ).wait_recv()

    pltpu.make_async_remote_copy(
        src_ref=kvg_pair.at[c],
        dst_ref=kvg_pair.at[1 - c],
        send_sem=kvg_sem.at[0],
        recv_sem=kvg_sem.at[1],
        device_id={"head": sibling},
        device_id_type=MESH,
    ).wait_recv()

    def z_copy(i, e, to_z):
        return pltpu.make_async_remote_copy(
            src_ref=z_out.at[i, e],
            dst_ref=z_in.at[z, e % PIECES],
            send_sem=z_send.at[i, e],
            recv_sem=z_recv.at[z, e % PIECES],
            device_id={"group": to_z, "head": y * CORES + e // PIECES},
            device_id_type=MESH,
        )

    for n, (i, e) in enumerate(chunks):
        b = lax.rem(z + 1 + i, per_half)
        to_z = c * per_half + b
        at = pl.multiple_of(b * wide, wide)
        acc = q_term(y, b, e)
        kvg_piece = kvg_pair[e // PIECES, pl.ds(e % PIECES * piece, piece), :]
        acc = acc + dot_nt(kvg_piece, wkv_half[pl.ds(at, wide), :])
        for k in range(1, chips):
            part_copies[k, i, e].wait_recv()
            acc = acc + part_in[k - 1, i, e].astype(F32)
        z_out[i, e] = acc.astype(BF16)
        away = jnp.logical_or(to_z != z, e // PIECES != c)

        @pl.when(away)
        def _():
            z_copy(i, e, to_z).start()

        @pl.when(jnp.logical_not(away))
        def _():
            z_in[z, e % PIECES] = z_out[i, e]

        if n + AHEAD < len(chunks):
            for k in range(1, chips):
                part_copies[k, i, e].wait_send()
            send_part(*chunks[n + AHEAD])

    source_core = z // per_half
    for p in range(PIECES):
        result = None
        for source in range(groups):

            @pl.when(jnp.logical_or(source != z, source_core != c))
            def _():
                pltpu.make_async_remote_copy(
                    src_ref=z_out.at[0, 0],
                    dst_ref=z_in.at[source, p],
                    send_sem=z_send.at[0, 0],
                    recv_sem=z_recv.at[source, p],
                    device_id={"head": sibling},
                    device_id_type=MESH,
                ).wait_recv()

            term = z_in[source, p].astype(F32)
            result = term if result is None else result + term
        out_ref[p * piece : (p + 1) * piece, :] = result.astype(BF16)

    for j in range(owners):

        @pl.when(CORES * j + my_half != h)
        def _():
            wkv_copy(j).wait_send()

    for copy in [w_copy, *dq_copies, kvg_copy, *near_copies, *dkv_copies]:
        copy.wait_send()
    for i, e in chunks[-AHEAD:]:
        for k in range(1, chips):
            part_copies[k, i, e].wait_send()
    for i, e in chunks:
        to_z = c * per_half + lax.rem(z + 1 + i, per_half)

        @pl.when(jnp.logical_or(to_z != z, e // PIECES != c))
        def _():
            z_copy(i, e, to_z).wait_send()


def shards(groups, heads, *args):
    query, kv, q_weight, kv_weight = args[0], args[2], args[6], args[8]
    seq, size = query.shape
    model = q_weight.shape[0]
    chips = heads // CORES
    tokens = seq // heads
    piece = tokens // PIECES
    wide = model // groups
    half = model // CORES
    per_half = groups // CORES
    owners = heads // CORES
    dma = pltpu.SemaphoreType.DMA
    vmem = pl.BlockSpec(memory_space=pltpu.VMEM)
    return pl.pallas_call(
        functools.partial(kernel, groups, heads),
        out_shape=(
            pltpu.VMEM((tokens, wide), BF16),
            pltpu.VMEM((tokens, 2 * size), BF16),
        ),
        in_specs=[pl.BlockSpec(memory_space=pltpu.HBM)] * ARGS,
        out_specs=(vmem, vmem),
        scratch_shapes=[pltpu.VMEM(arg.shape, arg.dtype) for arg in args]
        + [
            dma((ARGS,)),
            pltpu.VMEM((half, 2 * size), BF16),
            pltpu.VMEM((half, size), BF16),
            pltpu.VMEM((half, 2 * size), BF16),
            pltpu.VMEM(kv_weight.shape, BF16),
            pltpu.VMEM((seq, 2 * size), BF16),
            pltpu.VMEM((seq, 2 * size), BF16),
            pltpu.VMEM((chips, tokens, 2 * size), BF16),
            pltpu.VMEM((chips - 1, tokens, 2 * size), BF16),
            pltpu.VMEM((chips - 1, tokens, 2 * size), BF16),
            pltpu.VMEM((CORES, tokens, 2 * size), BF16),
            pltpu.VMEM((chips - 1, per_half, CORES * PIECES, piece, wide), BF16),
            pltpu.VMEM((chips - 1, per_half, CORES * PIECES, piece, wide), BF16),
            pltpu.VMEM((per_half, CORES * PIECES, piece, wide), BF16),
            pltpu.VMEM((groups, PIECES, piece, wide), BF16),
            pltpu.VMEM((seq, size), F32),
            pltpu.VMEM((seq, size), F32),
            dma((2,)),
            dma((owners,)),
            dma((owners,)),
            dma((chips,)),
            dma((chips,)),
            dma((chips,)),
            dma((chips,)),
            dma((chips - 1,)),
            dma((chips - 1,)),
            dma((2,)),
            dma((chips - 1, per_half, CORES * PIECES)),
            dma((chips - 1, per_half, CORES * PIECES)),
            dma((per_half, CORES * PIECES)),
            dma((groups, PIECES)),
        ],
        compiler_params=pltpu.CompilerParams(
            collective_id=0, has_side_effects=True, vmem_limit_bytes=55 * 1024 * 1024
        ),
    )(*args)


def solution(mesh):
    return jax.shard_map(
        functools.partial(shards, mesh.shape["group"], mesh.shape["head"]),
        mesh=mesh,
        in_specs=(
            P("dp", ("group", "head")),
            P(("group", "head"), "dp"),
            P("dp", "group"),
            P("group", "dp"),
            P("dp", ("group", "head")),
            P(("group", "head"), "dp"),
            P("dp", ("group", "head")),
            P("dp", ("group", "head")),
            P(("dp", "head"), "group"),
            P(("dp", "head"), "group"),
        ),
        out_specs=(P(("dp", "head"), "group"), P(("dp", "head"), "group")),
        check_vma=False,
    )
```

```python
import functools

import jax
import jax.numpy as jnp
from jax import lax
from jax.experimental import pallas as pl
from jax.experimental.pallas import tpu as pltpu
from jax.sharding import PartitionSpec as P

MESH = pl.DeviceIdType.MESH
F32 = jnp.float32
BF16 = jnp.bfloat16
CORES = 2
BLOCK = 32
LOG2_E = 1.4426950408889634
ARGS = 10
PIECES = 2
AHEAD = 4
LOAD_ORDER = (8, 9, 6, 7, 0, 1, 2, 3, 4, 5)


def power_of_two(exponent):
    scale = jnp.where(exponent == 0, 1.0, 0.0)
    for level in (-4, -3, -2, -1, 1, 2, 3, 4):
        scale = jnp.where(exponent == level, 2.0**level, scale)
    return scale.astype(F32)


def dequant_rows(mantissa, exponent):
    blocks, rows = exponent.shape
    scale = jnp.broadcast_to(power_of_two(exponent)[:, None, :], (blocks, BLOCK, rows))
    scale = scale.reshape(blocks * BLOCK, rows).T
    return (mantissa.astype(F32) * scale).astype(BF16)


def dequant_cols(mantissa, exponent):
    blocks, columns = exponent.shape
    scale = jnp.broadcast_to(power_of_two(exponent)[:, None, :], (blocks, BLOCK, columns))
    return (mantissa.astype(F32) * scale.reshape(blocks * BLOCK, columns)).astype(BF16)


def dot_nt(a, b):
    return lax.dot_general(a, b, (((1,), (1,)), ((), ())), preferred_element_type=F32)


def dot_tn(a, b):
    return lax.dot_general(a, b, (((0,), (0,)), ((), ())), preferred_element_type=F32)


def kernel(
    groups,
    heads,
    *refs,
):
    sources, (out_ref, kvg_ref) = refs[:ARGS], refs[ARGS : ARGS + 2]
    held = refs[ARGS + 2 : 2 * ARGS + 2]
    q_ref, qe_ref, kv_ref, kve_ref, do_ref, doe_ref, wq_ref, wqe_ref, wkv_ref, wkve_ref = held
    (
        load_sem,
        wq_pair,
        wq_out,
        wkv_half,
        wkv_out,
        dq_pair,
        dkv_out,
        dkv_near,
        dkv_sum,
        dkv_in,
        kvg_pair,
        part_out,
        part_in,
        z_out,
        z_in,
        dk_acc,
        dv_acc,
        w_sem,
        wkv_send,
        wkv_recv,
        dq_send,
        dq_recv,
        near_send,
        near_recv,
        dkv_send,
        dkv_recv,
        kvg_sem,
        part_send,
        part_recv,
        z_send,
        z_recv,
    ) = refs[2 * ARGS + 2 :]
    seq, size = q_ref.shape
    model = wq_ref.shape[0]
    chips = heads // CORES
    tokens = seq // heads
    wide = model // groups
    half = model // CORES
    per_half = groups // CORES
    piece = tokens // PIECES
    rows = wkv_ref.shape[0]
    owners = heads // CORES
    scale = 1.0 / size**0.5

    z = lax.axis_index("group")
    h = lax.axis_index("head")
    y = h // CORES
    c = lax.rem(h, CORES)
    sibling = y * CORES + (1 - c)

    loads = [
        pltpu.make_async_copy(source, held[at], load_sem.at[at])
        for at, source in enumerate(sources)
    ]
    for at in LOAD_ORDER:
        loads[at].start()

    barrier = pltpu.get_barrier_semaphore()
    for k in range(1, heads):
        pl.semaphore_signal(
            barrier, inc=1, device_id={"head": lax.rem(h + k, heads)}, device_id_type=MESH
        )
    for k in range(1, groups):
        for core in range(CORES):
            pl.semaphore_signal(
                barrier,
                inc=1,
                device_id={"group": lax.rem(z + k, groups), "head": y * CORES + core},
                device_id_type=MESH,
            )

    def weight_rows(which):
        first = pl.multiple_of(which * half, half)
        first_e = pl.multiple_of(which * (half // BLOCK), half // BLOCK)
        return dequant_cols(
            wq_ref[pl.ds(first, half), :], wqe_ref[pl.ds(first_e, half // BLOCK), :]
        )

    for at in LOAD_ORDER[:2]:
        loads[at].wait()
    wkv_out[...] = dequant_cols(wkv_ref[...], wkve_ref[...])
    pl.semaphore_wait(barrier, heads - 1 + CORES * (groups - 1))

    my_half = h // owners
    my_slot = pl.multiple_of(lax.rem(h, owners) * rows, rows)

    def wkv_copy(j):
        return pltpu.make_async_remote_copy(
            src_ref=wkv_out,
            dst_ref=wkv_half.at[pl.ds(my_slot, rows)],
            send_sem=wkv_send.at[j],
            recv_sem=wkv_recv.at[lax.rem(h, owners)],
            device_id={"head": CORES * j + my_half},
            device_id_type=MESH,
        )

    for j in range(owners):

        @pl.when(CORES * j + my_half != h)
        def _():
            wkv_copy(j).start()

    for at in LOAD_ORDER[2:4]:
        loads[at].wait()
    wq_out[...] = weight_rows(1 - c)
    w_copy = pltpu.make_async_remote_copy(
        src_ref=wq_out,
        dst_ref=wq_pair.at[:, size:],
        send_sem=w_sem.at[0],
        recv_sem=w_sem.at[1],
        device_id={"head": sibling},
        device_id_type=MESH,
    )
    w_copy.start()
    wq_pair[:, :size] = weight_rows(c)

    @pl.when(my_half == c)
    def _():
        wkv_half[pl.ds(my_slot, rows), :] = wkv_out[...]

    for at in LOAD_ORDER[4:]:
        loads[at].wait()
    query = dequant_rows(q_ref[...], qe_ref[...])
    kv = dequant_rows(kv_ref[...], kve_ref[...])
    grad = dequant_rows(do_ref[...], doe_ref[...])
    keys, values = kv[:, :size], kv[:, size:]
    block = CORES * tokens
    visible = lax.broadcasted_iota(jnp.int32, (block, block), 0) <= lax.broadcasted_iota(
        jnp.int32, (block, block), 1
    )
    dq_copies = []
    for index in reversed(range(chips)):
        first, upper = index * block, (index + 1) * block
        q_block, do_block = query[first:upper], grad[first:upper]
        spans = [(first, upper)] + ([(0, first)] if first else [])
        scores = [dot_nt(keys[lo:hi], q_block) for lo, hi in spans]
        scores[0] = jnp.where(visible, scores[0], -jnp.inf)
        peak = functools.reduce(
            jnp.maximum, [jnp.max(part, axis=0, keepdims=True) for part in scores]
        )
        expd = [jnp.exp2((part - peak) * (scale * LOG2_E)) for part in scores]
        total = sum(jnp.sum(part, axis=0, keepdims=True) for part in expd)
        inverse = 1.0 / total
        probs = [part * inverse for part in expd]
        dprob = [dot_nt(values[lo:hi], do_block) for lo, hi in spans]
        delta = sum(
            jnp.sum(p * dp, axis=0, keepdims=True) for p, dp in zip(probs, dprob)
        )
        dscore = [(p * (dp - delta)).astype(BF16) for p, dp in zip(probs, dprob)]
        dq = sum(dot_tn(part, keys[lo:hi]) for part, (lo, hi) in zip(dscore, spans))
        dq_pair[first:upper, :size] = (dq * scale).astype(BF16)
        copy = pltpu.make_async_remote_copy(
            src_ref=dq_pair.at[first:upper, :size],
            dst_ref=dq_pair.at[first:upper, size:],
            send_sem=dq_send.at[index],
            recv_sem=dq_recv.at[index],
            device_id={"head": sibling},
            device_id_type=MESH,
        )
        copy.start()
        dq_copies.append(copy)
        for part, p, (lo, hi) in zip(dscore, probs, spans):
            dk = jnp.dot(part, q_block, preferred_element_type=F32)
            dv = jnp.dot(p.astype(BF16), do_block, preferred_element_type=F32)
            if upper == seq:
                dk_acc[lo:hi, :] = dk
                dv_acc[lo:hi, :] = dv
            else:
                dk_acc[lo:hi, :] += dk
                dv_acc[lo:hi, :] += dv

    dkv_out[:, :size] = (dk_acc[...] * scale).astype(BF16)
    dkv_out[:, size:] = dv_acc[...].astype(BF16)

    def chip_rows(chip, core):
        return pl.ds(pl.multiple_of((chip * CORES + core) * tokens, tokens), tokens)

    near_copies = []
    for k in [*range(1, chips), 0]:
        copy = pltpu.make_async_remote_copy(
            src_ref=dkv_out.at[chip_rows(lax.rem(y + k, chips), 1 - c)],
            dst_ref=dkv_near.at[k],
            send_sem=near_send.at[k],
            recv_sem=near_recv.at[k],
            device_id={"head": sibling},
            device_id_type=MESH,
        )
        copy.start()
        near_copies.append(copy)
    def q_term(chip, b, e):
        first = pl.multiple_of(chip * CORES * tokens + e * piece, piece)
        at = pl.multiple_of(b * wide, wide)
        return dot_nt(dq_pair[pl.ds(first, piece), :], wq_pair[pl.ds(at, wide), :])

    w_copy.wait_recv()
    for copy in dq_copies:
        copy.wait_recv()
    chunks = [
        (i, core * PIECES + p)
        for i in range(per_half)
        for p in range(PIECES)
        for core in range(CORES)
    ]
    part_copies = {}

    def send_part(i, e):
        b = lax.rem(z + 1 + i, per_half)
        for k in range(1, chips):
            to = lax.rem(y + k, chips)
            part_out[k - 1, i, e] = q_term(to, b, e).astype(BF16)
            copy = pltpu.make_async_remote_copy(
                src_ref=part_out.at[k - 1, i, e],
                dst_ref=part_in.at[k - 1, i, e],
                send_sem=part_send.at[k - 1, i, e],
                recv_sem=part_recv.at[k - 1, i, e],
                device_id={"head": to * CORES + c},
                device_id_type=MESH,
            )
            copy.start()
            part_copies[k, i, e] = copy

    for i, e in chunks[: AHEAD // 2]:
        send_part(i, e)

    dkv_copies = []
    for k in range(1, chips):
        to = lax.rem(y + k, chips)
        near_copies[k - 1].wait_recv()
        both = dkv_out[chip_rows(to, c), :].astype(F32) + dkv_near[k].astype(F32)
        dkv_sum[k - 1] = both.astype(BF16)
        copy = pltpu.make_async_remote_copy(
            src_ref=dkv_sum.at[k - 1],
            dst_ref=dkv_in.at[k - 1],
            send_sem=dkv_send.at[k - 1],
            recv_sem=dkv_recv.at[k - 1],
            device_id={"head": to * CORES + c},
            device_id_type=MESH,
        )
        copy.start()
        dkv_copies.append(copy)

    for i, e in chunks[AHEAD // 2 : AHEAD]:
        send_part(i, e)

    near_copies[-1].wait_recv()
    total = dkv_out[chip_rows(y, c), :].astype(F32) + dkv_near[0].astype(F32)
    for k in range(1, chips):
        dkv_copies[k - 1].wait_recv()
        total = total + dkv_in[k - 1].astype(F32)
    kvg = total.astype(BF16)
    kvg_ref[...] = kvg
    kvg_pair[c] = kvg
    kvg_copy = pltpu.make_async_remote_copy(
        src_ref=kvg_pair.at[c],
        dst_ref=kvg_pair.at[c],
        send_sem=kvg_sem.at[0],
        recv_sem=kvg_sem.at[1],
        device_id={"head": sibling},
        device_id_type=MESH,
    )
    kvg_copy.start()
    for s in range(owners):

        @pl.when(c * owners + s != h)
        def _():
            pltpu.make_async_remote_copy(
                src_ref=wkv_out,
                dst_ref=wkv_half.at[pl.ds(s * rows, rows)],
                send_sem=wkv_send.at[s],
                recv_sem=wkv_recv.at[s],
                device_id={"head": sibling},
                device_id_type=MESH,
            ).wait_recv()

    pltpu.make_async_remote_copy(
        src_ref=kvg_pair.at[c],
        dst_ref=kvg_pair.at[1 - c],
        send_sem=kvg_sem.at[0],
        recv_sem=kvg_sem.at[1],
        device_id={"head": sibling},
        device_id_type=MESH,
    ).wait_recv()

    def z_copy(i, e, to_z):
        return pltpu.make_async_remote_copy(
            src_ref=z_out.at[i, e],
            dst_ref=z_in.at[z, e % PIECES],
            send_sem=z_send.at[i, e],
            recv_sem=z_recv.at[z, e % PIECES],
            device_id={"group": to_z, "head": y * CORES + e // PIECES},
            device_id_type=MESH,
        )

    for n, (i, e) in enumerate(chunks):
        b = lax.rem(z + 1 + i, per_half)
        to_z = c * per_half + b
        at = pl.multiple_of(b * wide, wide)
        acc = q_term(y, b, e)
        kvg_piece = kvg_pair[e // PIECES, pl.ds(e % PIECES * piece, piece), :]
        acc = acc + dot_nt(kvg_piece, wkv_half[pl.ds(at, wide), :])
        for k in range(1, chips):
            part_copies[k, i, e].wait_recv()
            acc = acc + part_in[k - 1, i, e].astype(F32)
        z_out[i, e] = acc.astype(BF16)
        away = jnp.logical_or(to_z != z, e // PIECES != c)

        @pl.when(away)
        def _():
            z_copy(i, e, to_z).start()

        @pl.when(jnp.logical_not(away))
        def _():
            z_in[z, e % PIECES] = z_out[i, e]

        if n + AHEAD < len(chunks):
            for k in range(1, chips):
                part_copies[k, i, e].wait_send()
            send_part(*chunks[n + AHEAD])

    source_core = z // per_half
    for p in range(PIECES):
        result = None
        for source in range(groups):

            @pl.when(jnp.logical_or(source != z, source_core != c))
            def _():
                pltpu.make_async_remote_copy(
                    src_ref=z_out.at[0, 0],
                    dst_ref=z_in.at[source, p],
                    send_sem=z_send.at[0, 0],
                    recv_sem=z_recv.at[source, p],
                    device_id={"head": sibling},
                    device_id_type=MESH,
                ).wait_recv()

            term = z_in[source, p].astype(F32)
            result = term if result is None else result + term
        out_ref[p * piece : (p + 1) * piece, :] = result.astype(BF16)

    for j in range(owners):

        @pl.when(CORES * j + my_half != h)
        def _():
            wkv_copy(j).wait_send()

    for copy in [w_copy, *dq_copies, kvg_copy, *near_copies, *dkv_copies]:
        copy.wait_send()
    for i, e in chunks[-AHEAD:]:
        for k in range(1, chips):
            part_copies[k, i, e].wait_send()
    for i, e in chunks:
        to_z = c * per_half + lax.rem(z + 1 + i, per_half)

        @pl.when(jnp.logical_or(to_z != z, e // PIECES != c))
        def _():
            z_copy(i, e, to_z).wait_send()


def shards(groups, heads, *args):
    query, kv, q_weight, kv_weight = args[0], args[2], args[6], args[8]
    seq, size = query.shape
    model = q_weight.shape[0]
    chips = heads // CORES
    tokens = seq // heads
    piece = tokens // PIECES
    wide = model // groups
    half = model // CORES
    per_half = groups // CORES
    owners = heads // CORES
    dma = pltpu.SemaphoreType.DMA
    vmem = pl.BlockSpec(memory_space=pltpu.VMEM)
    return pl.pallas_call(
        functools.partial(kernel, groups, heads),
        out_shape=(
            pltpu.VMEM((tokens, wide), BF16),
            pltpu.VMEM((tokens, 2 * size), BF16),
        ),
        in_specs=[pl.BlockSpec(memory_space=pltpu.HBM)] * ARGS,
        out_specs=(vmem, vmem),
        scratch_shapes=[pltpu.VMEM(arg.shape, arg.dtype) for arg in args]
        + [
            dma((ARGS,)),
            pltpu.VMEM((half, 2 * size), BF16),
            pltpu.VMEM((half, size), BF16),
            pltpu.VMEM((half, 2 * size), BF16),
            pltpu.VMEM(kv_weight.shape, BF16),
            pltpu.VMEM((seq, 2 * size), BF16),
            pltpu.VMEM((seq, 2 * size), BF16),
            pltpu.VMEM((chips, tokens, 2 * size), BF16),
            pltpu.VMEM((chips - 1, tokens, 2 * size), BF16),
            pltpu.VMEM((chips - 1, tokens, 2 * size), BF16),
            pltpu.VMEM((CORES, tokens, 2 * size), BF16),
            pltpu.VMEM((chips - 1, per_half, CORES * PIECES, piece, wide), BF16),
            pltpu.VMEM((chips - 1, per_half, CORES * PIECES, piece, wide), BF16),
            pltpu.VMEM((per_half, CORES * PIECES, piece, wide), BF16),
            pltpu.VMEM((groups, PIECES, piece, wide), BF16),
            pltpu.VMEM((seq, size), F32),
            pltpu.VMEM((seq, size), F32),
            dma((2,)),
            dma((owners,)),
            dma((owners,)),
            dma((chips,)),
            dma((chips,)),
            dma((chips,)),
            dma((chips,)),
            dma((chips - 1,)),
            dma((chips - 1,)),
            dma((2,)),
            dma((chips - 1, per_half, CORES * PIECES)),
            dma((chips - 1, per_half, CORES * PIECES)),
            dma((per_half, CORES * PIECES)),
            dma((groups, PIECES)),
        ],
        compiler_params=pltpu.CompilerParams(
            collective_id=0, has_side_effects=True, vmem_limit_bytes=55 * 1024 * 1024
        ),
    )(*args)


def solution(mesh):
    return jax.shard_map(
        functools.partial(shards, mesh.shape["group"], mesh.shape["head"]),
        mesh=mesh,
        in_specs=(
            P("dp", ("group", "head")),
            P(("group", "head"), "dp"),
            P("dp", "group"),
            P("group", "dp"),
            P("dp", ("group", "head")),
            P(("group", "head"), "dp"),
            P("dp", ("group", "head")),
            P("dp", ("group", "head")),
            P(("dp", "head"), "group"),
            P(("dp", "head"), "group"),
        ),
        out_specs=(P(("dp", "head"), "group"), P(("dp", "head"), "group")),
        check_vma=False,
    )
```

```python
import functools

import jax
import jax.numpy as jnp
from jax import lax
from jax.experimental import pallas as pl
from jax.experimental.pallas import tpu as pltpu
from jax.sharding import PartitionSpec as P

MESH = pl.DeviceIdType.MESH
F32 = jnp.float32
BF16 = jnp.bfloat16
CORES = 2
BLOCK = 32
LOG2_E = 1.4426950408889634
ARGS = 10
PIECES = 2
AHEAD = 4
LOAD_ORDER = (8, 9, 6, 7, 0, 1, 2, 3, 4, 5)


def power_of_two(exponent):
    scale = jnp.where(exponent == 0, 1.0, 0.0)
    for level in (-4, -3, -2, -1, 1, 2, 3, 4):
        scale = jnp.where(exponent == level, 2.0**level, scale)
    return scale.astype(F32)


def dequant_rows(mantissa, exponent):
    blocks, rows = exponent.shape
    scale = jnp.broadcast_to(power_of_two(exponent)[:, None, :], (blocks, BLOCK, rows))
    scale = scale.reshape(blocks * BLOCK, rows).T
    return (mantissa.astype(F32) * scale).astype(BF16)


def dequant_cols(mantissa, exponent):
    blocks, columns = exponent.shape
    scale = jnp.broadcast_to(power_of_two(exponent)[:, None, :], (blocks, BLOCK, columns))
    return (mantissa.astype(F32) * scale.reshape(blocks * BLOCK, columns)).astype(BF16)


def dot_nt(a, b):
    return lax.dot_general(a, b, (((1,), (1,)), ((), ())), preferred_element_type=F32)


def dot_tn(a, b):
    return lax.dot_general(a, b, (((0,), (0,)), ((), ())), preferred_element_type=F32)


def kernel(
    groups,
    heads,
    *refs,
):
    sources, (out_ref, kvg_ref) = refs[:ARGS], refs[ARGS : ARGS + 2]
    held = refs[ARGS + 2 : 2 * ARGS + 2]
    q_ref, qe_ref, kv_ref, kve_ref, do_ref, doe_ref, wq_ref, wqe_ref, wkv_ref, wkve_ref = held
    (
        load_sem,
        wq_pair,
        wq_out,
        wkv_half,
        wkv_out,
        dq_pair,
        dkv_out,
        dkv_near,
        dkv_sum,
        dkv_in,
        kvg_pair,
        part_out,
        part_in,
        z_out,
        z_in,
        dk_acc,
        dv_acc,
        w_sem,
        wkv_send,
        wkv_recv,
        dq_send,
        dq_recv,
        near_send,
        near_recv,
        dkv_send,
        dkv_recv,
        kvg_sem,
        part_send,
        part_recv,
        z_send,
        z_recv,
    ) = refs[2 * ARGS + 2 :]
    seq, size = q_ref.shape
    model = wq_ref.shape[0]
    chips = heads // CORES
    tokens = seq // heads
    wide = model // groups
    half = model // CORES
    per_half = groups // CORES
    piece = tokens // PIECES
    rows = wkv_ref.shape[0]
    owners = heads // CORES
    scale = 1.0 / size**0.5

    z = lax.axis_index("group")
    h = lax.axis_index("head")
    y = h // CORES
    c = lax.rem(h, CORES)
    sibling = y * CORES + (1 - c)

    loads = [
        pltpu.make_async_copy(source, held[at], load_sem.at[at])
        for at, source in enumerate(sources)
    ]
    for at in LOAD_ORDER:
        loads[at].start()

    barrier = pltpu.get_barrier_semaphore()
    for k in range(1, heads):
        pl.semaphore_signal(
            barrier, inc=1, device_id={"head": lax.rem(h + k, heads)}, device_id_type=MESH
        )
    for k in range(1, groups):
        for core in range(CORES):
            pl.semaphore_signal(
                barrier,
                inc=1,
                device_id={"group": lax.rem(z + k, groups), "head": y * CORES + core},
                device_id_type=MESH,
            )

    def weight_rows(which):
        first = pl.multiple_of(which * half, half)
        first_e = pl.multiple_of(which * (half // BLOCK), half // BLOCK)
        return dequant_cols(
            wq_ref[pl.ds(first, half), :], wqe_ref[pl.ds(first_e, half // BLOCK), :]
        )

    for at in LOAD_ORDER[:2]:
        loads[at].wait()
    wkv_out[...] = dequant_cols(wkv_ref[...], wkve_ref[...])
    pl.semaphore_wait(barrier, heads - 1 + CORES * (groups - 1))

    my_half = h // owners
    my_slot = pl.multiple_of(lax.rem(h, owners) * rows, rows)

    def wkv_copy(j):
        return pltpu.make_async_remote_copy(
            src_ref=wkv_out,
            dst_ref=wkv_half.at[pl.ds(my_slot, rows)],
            send_sem=wkv_send.at[j],
            recv_sem=wkv_recv.at[lax.rem(h, owners)],
            device_id={"head": CORES * j + my_half},
            device_id_type=MESH,
        )

    for j in range(owners):

        @pl.when(CORES * j + my_half != h)
        def _():
            wkv_copy(j).start()

    for at in LOAD_ORDER[2:4]:
        loads[at].wait()
    wq_out[...] = weight_rows(1 - c)
    w_copy = pltpu.make_async_remote_copy(
        src_ref=wq_out,
        dst_ref=wq_pair.at[:, size:],
        send_sem=w_sem.at[0],
        recv_sem=w_sem.at[1],
        device_id={"head": sibling},
        device_id_type=MESH,
    )
    w_copy.start()
    wq_pair[:, :size] = weight_rows(c)

    @pl.when(my_half == c)
    def _():
        wkv_half[pl.ds(my_slot, rows), :] = wkv_out[...]

    for at in LOAD_ORDER[4:]:
        loads[at].wait()
    query = dequant_rows(q_ref[...], qe_ref[...])
    kv = dequant_rows(kv_ref[...], kve_ref[...])
    grad = dequant_rows(do_ref[...], doe_ref[...])
    keys, values = kv[:, :size], kv[:, size:]
    block = CORES * tokens
    visible = lax.broadcasted_iota(jnp.int32, (block, block), 0) <= lax.broadcasted_iota(
        jnp.int32, (block, block), 1
    )
    dq_copies, near_copies = [], []

    def chip_rows(chip, core):
        return pl.ds(pl.multiple_of((chip * CORES + core) * tokens, tokens), tokens)

    for index in reversed(range(chips)):
        first, upper = index * block, (index + 1) * block
        q_block, do_block = query[first:upper], grad[first:upper]
        spans = [(first, upper)] + ([(0, first)] if first else [])
        scores = [dot_nt(keys[lo:hi], q_block) for lo, hi in spans]
        scores[0] = jnp.where(visible, scores[0], -jnp.inf)
        peak = functools.reduce(
            jnp.maximum, [jnp.max(part, axis=0, keepdims=True) for part in scores]
        )
        expd = [jnp.exp2((part - peak) * (scale * LOG2_E)) for part in scores]
        total = sum(jnp.sum(part, axis=0, keepdims=True) for part in expd)
        inverse = 1.0 / total
        probs = [part * inverse for part in expd]
        dprob = [dot_nt(values[lo:hi], do_block) for lo, hi in spans]
        delta = sum(
            jnp.sum(p * dp, axis=0, keepdims=True) for p, dp in zip(probs, dprob)
        )
        dscore = [(p * (dp - delta)).astype(BF16) for p, dp in zip(probs, dprob)]
        for part, p, (lo, hi) in zip(dscore, probs, spans):
            dk = jnp.dot(part, q_block, preferred_element_type=F32)
            dv = jnp.dot(p.astype(BF16), do_block, preferred_element_type=F32)
            if upper == seq:
                dk_acc[lo:hi, :] = dk
                dv_acc[lo:hi, :] = dv
            else:
                dk_acc[lo:hi, :] += dk
                dv_acc[lo:hi, :] += dv

        dkv_out[first:upper, :size] = (dk_acc[first:upper, :] * scale).astype(BF16)
        dkv_out[first:upper, size:] = dv_acc[first:upper, :].astype(BF16)
        copy = pltpu.make_async_remote_copy(
            src_ref=dkv_out.at[chip_rows(index, 1 - c)],
            dst_ref=dkv_near.at[index],
            send_sem=near_send.at[index],
            recv_sem=near_recv.at[index],
            device_id={"head": sibling},
            device_id_type=MESH,
        )
        copy.start()
        near_copies.append(copy)
        dq = sum(dot_tn(part, keys[lo:hi]) for part, (lo, hi) in zip(dscore, spans))
        dq_pair[first:upper, :size] = (dq * scale).astype(BF16)
        copy = pltpu.make_async_remote_copy(
            src_ref=dq_pair.at[first:upper, :size],
            dst_ref=dq_pair.at[first:upper, size:],
            send_sem=dq_send.at[index],
            recv_sem=dq_recv.at[index],
            device_id={"head": sibling},
            device_id_type=MESH,
        )
        copy.start()
        dq_copies.append(copy)

    for copy in near_copies:
        copy.wait_recv()
    dkv_copies = []
    for k in range(1, chips):
        to = lax.rem(y + k, chips)
        both = dkv_out[chip_rows(to, c), :].astype(F32) + dkv_near[to].astype(F32)
        dkv_sum[k - 1] = both.astype(BF16)
        copy = pltpu.make_async_remote_copy(
            src_ref=dkv_sum.at[k - 1],
            dst_ref=dkv_in.at[k - 1],
            send_sem=dkv_send.at[k - 1],
            recv_sem=dkv_recv.at[k - 1],
            device_id={"head": to * CORES + c},
            device_id_type=MESH,
        )
        copy.start()
        dkv_copies.append(copy)

    def q_term(chip, b, e):
        first = pl.multiple_of(chip * CORES * tokens + e * piece, piece)
        at = pl.multiple_of(b * wide, wide)
        return dot_nt(dq_pair[pl.ds(first, piece), :], wq_pair[pl.ds(at, wide), :])

    w_copy.wait_recv()
    for copy in dq_copies:
        copy.wait_recv()
    chunks = [
        (i, core * PIECES + p)
        for i in range(per_half)
        for p in range(PIECES)
        for core in range(CORES)
    ]
    part_copies = {}

    def send_part(i, e):
        b = lax.rem(z + 1 + i, per_half)
        for k in range(1, chips):
            to = lax.rem(y + k, chips)
            part_out[k - 1, i, e] = q_term(to, b, e).astype(BF16)
            copy = pltpu.make_async_remote_copy(
                src_ref=part_out.at[k - 1, i, e],
                dst_ref=part_in.at[k - 1, i, e],
                send_sem=part_send.at[k - 1, i, e],
                recv_sem=part_recv.at[k - 1, i, e],
                device_id={"head": to * CORES + c},
                device_id_type=MESH,
            )
            copy.start()
            part_copies[k, i, e] = copy

    for i, e in chunks[:AHEAD]:
        send_part(i, e)

    total = dkv_out[chip_rows(y, c), :].astype(F32) + dkv_near[y].astype(F32)
    for k in range(1, chips):
        dkv_copies[k - 1].wait_recv()
        total = total + dkv_in[k - 1].astype(F32)
    kvg = total.astype(BF16)
    kvg_ref[...] = kvg
    kvg_pair[c] = kvg
    kvg_copy = pltpu.make_async_remote_copy(
        src_ref=kvg_pair.at[c],
        dst_ref=kvg_pair.at[c],
        send_sem=kvg_sem.at[0],
        recv_sem=kvg_sem.at[1],
        device_id={"head": sibling},
        device_id_type=MESH,
    )
    kvg_copy.start()
    for s in range(owners):

        @pl.when(c * owners + s != h)
        def _():
            pltpu.make_async_remote_copy(
                src_ref=wkv_out,
                dst_ref=wkv_half.at[pl.ds(s * rows, rows)],
                send_sem=wkv_send.at[s],
                recv_sem=wkv_recv.at[s],
                device_id={"head": sibling},
                device_id_type=MESH,
            ).wait_recv()

    pltpu.make_async_remote_copy(
        src_ref=kvg_pair.at[c],
        dst_ref=kvg_pair.at[1 - c],
        send_sem=kvg_sem.at[0],
        recv_sem=kvg_sem.at[1],
        device_id={"head": sibling},
        device_id_type=MESH,
    ).wait_recv()

    def z_copy(i, e, to_z):
        return pltpu.make_async_remote_copy(
            src_ref=z_out.at[i, e],
            dst_ref=z_in.at[z, e % PIECES],
            send_sem=z_send.at[i, e],
            recv_sem=z_recv.at[z, e % PIECES],
            device_id={"group": to_z, "head": y * CORES + e // PIECES},
            device_id_type=MESH,
        )

    for n, (i, e) in enumerate(chunks):
        b = lax.rem(z + 1 + i, per_half)
        to_z = c * per_half + b
        at = pl.multiple_of(b * wide, wide)
        acc = q_term(y, b, e)
        kvg_piece = kvg_pair[e // PIECES, pl.ds(e % PIECES * piece, piece), :]
        acc = acc + dot_nt(kvg_piece, wkv_half[pl.ds(at, wide), :])
        for k in range(1, chips):
            part_copies[k, i, e].wait_recv()
            acc = acc + part_in[k - 1, i, e].astype(F32)
        z_out[i, e] = acc.astype(BF16)
        away = jnp.logical_or(to_z != z, e // PIECES != c)

        @pl.when(away)
        def _():
            z_copy(i, e, to_z).start()

        @pl.when(jnp.logical_not(away))
        def _():
            z_in[z, e % PIECES] = z_out[i, e]

        if n + AHEAD < len(chunks):
            for k in range(1, chips):
                part_copies[k, i, e].wait_send()
            send_part(*chunks[n + AHEAD])

    source_core = z // per_half
    for p in range(PIECES):
        result = None
        for source in range(groups):

            @pl.when(jnp.logical_or(source != z, source_core != c))
            def _():
                pltpu.make_async_remote_copy(
                    src_ref=z_out.at[0, 0],
                    dst_ref=z_in.at[source, p],
                    send_sem=z_send.at[0, 0],
                    recv_sem=z_recv.at[source, p],
                    device_id={"head": sibling},
                    device_id_type=MESH,
                ).wait_recv()

            term = z_in[source, p].astype(F32)
            result = term if result is None else result + term
        out_ref[p * piece : (p + 1) * piece, :] = result.astype(BF16)

    for j in range(owners):

        @pl.when(CORES * j + my_half != h)
        def _():
            wkv_copy(j).wait_send()

    for copy in [w_copy, *dq_copies, kvg_copy, *near_copies, *dkv_copies]:
        copy.wait_send()
    for i, e in chunks[-AHEAD:]:
        for k in range(1, chips):
            part_copies[k, i, e].wait_send()
    for i, e in chunks:
        to_z = c * per_half + lax.rem(z + 1 + i, per_half)

        @pl.when(jnp.logical_or(to_z != z, e // PIECES != c))
        def _():
            z_copy(i, e, to_z).wait_send()


def shards(groups, heads, *args):
    query, kv, q_weight, kv_weight = args[0], args[2], args[6], args[8]
    seq, size = query.shape
    model = q_weight.shape[0]
    chips = heads // CORES
    tokens = seq // heads
    piece = tokens // PIECES
    wide = model // groups
    half = model // CORES
    per_half = groups // CORES
    owners = heads // CORES
    dma = pltpu.SemaphoreType.DMA
    vmem = pl.BlockSpec(memory_space=pltpu.VMEM)
    return pl.pallas_call(
        functools.partial(kernel, groups, heads),
        out_shape=(
            pltpu.VMEM((tokens, wide), BF16),
            pltpu.VMEM((tokens, 2 * size), BF16),
        ),
        in_specs=[pl.BlockSpec(memory_space=pltpu.HBM)] * ARGS,
        out_specs=(vmem, vmem),
        scratch_shapes=[pltpu.VMEM(arg.shape, arg.dtype) for arg in args]
        + [
            dma((ARGS,)),
            pltpu.VMEM((half, 2 * size), BF16),
            pltpu.VMEM((half, size), BF16),
            pltpu.VMEM((half, 2 * size), BF16),
            pltpu.VMEM(kv_weight.shape, BF16),
            pltpu.VMEM((seq, 2 * size), BF16),
            pltpu.VMEM((seq, 2 * size), BF16),
            pltpu.VMEM((chips, tokens, 2 * size), BF16),
            pltpu.VMEM((chips - 1, tokens, 2 * size), BF16),
            pltpu.VMEM((chips - 1, tokens, 2 * size), BF16),
            pltpu.VMEM((CORES, tokens, 2 * size), BF16),
            pltpu.VMEM((chips - 1, per_half, CORES * PIECES, piece, wide), BF16),
            pltpu.VMEM((chips - 1, per_half, CORES * PIECES, piece, wide), BF16),
            pltpu.VMEM((per_half, CORES * PIECES, piece, wide), BF16),
            pltpu.VMEM((groups, PIECES, piece, wide), BF16),
            pltpu.VMEM((seq, size), F32),
            pltpu.VMEM((seq, size), F32),
            dma((2,)),
            dma((owners,)),
            dma((owners,)),
            dma((chips,)),
            dma((chips,)),
            dma((chips,)),
            dma((chips,)),
            dma((chips - 1,)),
            dma((chips - 1,)),
            dma((2,)),
            dma((chips - 1, per_half, CORES * PIECES)),
            dma((chips - 1, per_half, CORES * PIECES)),
            dma((per_half, CORES * PIECES)),
            dma((groups, PIECES)),
        ],
        compiler_params=pltpu.CompilerParams(
            collective_id=0, has_side_effects=True, vmem_limit_bytes=55 * 1024 * 1024
        ),
    )(*args)


def solution(mesh):
    return jax.shard_map(
        functools.partial(shards, mesh.shape["group"], mesh.shape["head"]),
        mesh=mesh,
        in_specs=(
            P("dp", ("group", "head")),
            P(("group", "head"), "dp"),
            P("dp", "group"),
            P("group", "dp"),
            P("dp", ("group", "head")),
            P(("group", "head"), "dp"),
            P("dp", ("group", "head")),
            P("dp", ("group", "head")),
            P(("dp", "head"), "group"),
            P(("dp", "head"), "group"),
        ),
        out_specs=(P(("dp", "head"), "group"), P(("dp", "head"), "group")),
        check_vma=False,
    )
```

```python
import functools

import jax
import jax.numpy as jnp
from jax import lax
from jax.experimental import pallas as pl
from jax.experimental.pallas import tpu as pltpu
from jax.sharding import PartitionSpec as P

MESH = pl.DeviceIdType.MESH
F32 = jnp.float32
BF16 = jnp.bfloat16
CORES = 2
BLOCK = 32
LOG2_E = 1.4426950408889634
ARGS = 10
PIECES = 2
AHEAD = 4
LOAD_ORDER = (8, 9, 6, 7, 0, 1, 2, 3, 4, 5)


def power_of_two(exponent):
    scale = jnp.where(exponent == 0, 1.0, 0.0)
    for level in (-4, -3, -2, -1, 1, 2, 3, 4):
        scale = jnp.where(exponent == level, 2.0**level, scale)
    return scale.astype(F32)


def dequant_rows(mantissa, exponent):
    blocks, rows = exponent.shape
    scale = jnp.broadcast_to(power_of_two(exponent)[:, None, :], (blocks, BLOCK, rows))
    scale = scale.reshape(blocks * BLOCK, rows).T
    return (mantissa.astype(F32) * scale).astype(BF16)


def dequant_cols(mantissa, exponent):
    blocks, columns = exponent.shape
    scale = jnp.broadcast_to(power_of_two(exponent)[:, None, :], (blocks, BLOCK, columns))
    return (mantissa.astype(F32) * scale.reshape(blocks * BLOCK, columns)).astype(BF16)


def dot_nt(a, b):
    return lax.dot_general(a, b, (((1,), (1,)), ((), ())), preferred_element_type=F32)


def dot_tn(a, b):
    return lax.dot_general(a, b, (((0,), (0,)), ((), ())), preferred_element_type=F32)


def kernel(
    groups,
    heads,
    *refs,
):
    sources, (out_ref, kvg_ref) = refs[:ARGS], refs[ARGS : ARGS + 2]
    held = refs[ARGS + 2 : 2 * ARGS + 2]
    q_ref, qe_ref, kv_ref, kve_ref, do_ref, doe_ref, wq_ref, wqe_ref, wkv_ref, wkve_ref = held
    (
        load_sem,
        wq_pair,
        wq_out,
        wkv_half,
        wkv_out,
        dq_pair,
        dkv_out,
        dkv_near,
        dkv_sum,
        dkv_in,
        kvg_pair,
        part_out,
        part_in,
        z_out,
        z_in,
        dk_acc,
        dv_acc,
        w_sem,
        wkv_send,
        wkv_recv,
        dq_send,
        dq_recv,
        near_send,
        near_recv,
        dkv_send,
        dkv_recv,
        kvg_sem,
        part_send,
        part_recv,
        z_send,
        z_recv,
    ) = refs[2 * ARGS + 2 :]
    seq, size = q_ref.shape
    model = wq_ref.shape[0]
    chips = heads // CORES
    tokens = seq // heads
    wide = model // groups
    half = model // CORES
    per_half = groups // CORES
    piece = tokens // PIECES
    rows = wkv_ref.shape[0]
    owners = heads // CORES
    scale = 1.0 / size**0.5

    z = lax.axis_index("group")
    h = lax.axis_index("head")
    y = h // CORES
    c = lax.rem(h, CORES)
    sibling = y * CORES + (1 - c)

    loads = [
        pltpu.make_async_copy(source, held[at], load_sem.at[at])
        for at, source in enumerate(sources)
    ]
    for at in LOAD_ORDER:
        loads[at].start()

    barrier = pltpu.get_barrier_semaphore()
    for k in range(1, heads):
        pl.semaphore_signal(
            barrier, inc=1, device_id={"head": lax.rem(h + k, heads)}, device_id_type=MESH
        )
    for k in range(1, groups):
        for core in range(CORES):
            pl.semaphore_signal(
                barrier,
                inc=1,
                device_id={"group": lax.rem(z + k, groups), "head": y * CORES + core},
                device_id_type=MESH,
            )

    def weight_rows(which):
        first = pl.multiple_of(which * half, half)
        first_e = pl.multiple_of(which * (half // BLOCK), half // BLOCK)
        return dequant_cols(
            wq_ref[pl.ds(first, half), :], wqe_ref[pl.ds(first_e, half // BLOCK), :]
        )

    for at in LOAD_ORDER[:2]:
        loads[at].wait()
    wkv_out[...] = dequant_cols(wkv_ref[...], wkve_ref[...])
    pl.semaphore_wait(barrier, heads - 1 + CORES * (groups - 1))

    my_half = h // owners
    my_owner = lax.rem(h, owners)
    my_slot = pl.multiple_of(my_owner * rows, rows)
    early = (my_owner * rows) // wide == lax.rem(z + 1, per_half)

    def wkv_copy(j, part):
        cut = rows // 2
        at = pl.multiple_of(my_owner * rows + part * cut, cut)
        return pltpu.make_async_remote_copy(
            src_ref=wkv_out.at[pl.ds(part * cut, cut)],
            dst_ref=wkv_half.at[pl.ds(at, cut)],
            send_sem=wkv_send.at[j, part],
            recv_sem=wkv_recv.at[my_owner, part],
            device_id={"head": CORES * j + my_half},
            device_id_type=MESH,
        )

    def send_wkv(part, now):
        for j in range(owners):

            @pl.when(jnp.logical_and(CORES * j + my_half != h, now))
            def _():
                wkv_copy(j, part).start()

    send_wkv(0, True)
    send_wkv(1, early)

    for at in LOAD_ORDER[2:4]:
        loads[at].wait()
    wq_out[...] = weight_rows(1 - c)
    w_copy = pltpu.make_async_remote_copy(
        src_ref=wq_out,
        dst_ref=wq_pair.at[:, size:],
        send_sem=w_sem.at[0],
        recv_sem=w_sem.at[1],
        device_id={"head": sibling},
        device_id_type=MESH,
    )
    w_copy.start()
    wq_pair[:, :size] = weight_rows(c)

    @pl.when(my_half == c)
    def _():
        wkv_half[pl.ds(my_slot, rows), :] = wkv_out[...]

    for at in LOAD_ORDER[4:]:
        loads[at].wait()
    query = dequant_rows(q_ref[...], qe_ref[...])
    kv = dequant_rows(kv_ref[...], kve_ref[...])
    grad = dequant_rows(do_ref[...], doe_ref[...])
    keys, values = kv[:, :size], kv[:, size:]
    block = CORES * tokens
    visible = lax.broadcasted_iota(jnp.int32, (block, block), 0) <= lax.broadcasted_iota(
        jnp.int32, (block, block), 1
    )
    dq_copies, near_copies = [], []

    def chip_rows(chip, core):
        return pl.ds(pl.multiple_of((chip * CORES + core) * tokens, tokens), tokens)

    for index in reversed(range(chips)):
        first, upper = index * block, (index + 1) * block
        q_block, do_block = query[first:upper], grad[first:upper]
        spans = [(first, upper)] + ([(0, first)] if first else [])
        scores = [dot_nt(keys[lo:hi], q_block) for lo, hi in spans]
        scores[0] = jnp.where(visible, scores[0], -jnp.inf)
        peak = functools.reduce(
            jnp.maximum, [jnp.max(part, axis=0, keepdims=True) for part in scores]
        )
        expd = [jnp.exp2((part - peak) * (scale * LOG2_E)) for part in scores]
        total = sum(jnp.sum(part, axis=0, keepdims=True) for part in expd)
        inverse = 1.0 / total
        probs = [part * inverse for part in expd]
        dprob = [dot_nt(values[lo:hi], do_block) for lo, hi in spans]
        delta = sum(
            jnp.sum(p * dp, axis=0, keepdims=True) for p, dp in zip(probs, dprob)
        )
        dscore = [(p * (dp - delta)).astype(BF16) for p, dp in zip(probs, dprob)]
        for part, p, (lo, hi) in zip(dscore, probs, spans):
            dk = jnp.dot(part, q_block, preferred_element_type=F32)
            dv = jnp.dot(p.astype(BF16), do_block, preferred_element_type=F32)
            if upper == seq:
                dk_acc[lo:hi, :] = dk
                dv_acc[lo:hi, :] = dv
            else:
                dk_acc[lo:hi, :] += dk
                dv_acc[lo:hi, :] += dv

        dkv_out[first:upper, :size] = (dk_acc[first:upper, :] * scale).astype(BF16)
        dkv_out[first:upper, size:] = dv_acc[first:upper, :].astype(BF16)
        copy = pltpu.make_async_remote_copy(
            src_ref=dkv_out.at[chip_rows(index, 1 - c)],
            dst_ref=dkv_near.at[index],
            send_sem=near_send.at[index],
            recv_sem=near_recv.at[index],
            device_id={"head": sibling},
            device_id_type=MESH,
        )
        copy.start()
        near_copies.append(copy)
        dq = sum(dot_tn(part, keys[lo:hi]) for part, (lo, hi) in zip(dscore, spans))
        dq_pair[first:upper, :size] = (dq * scale).astype(BF16)
        copy = pltpu.make_async_remote_copy(
            src_ref=dq_pair.at[first:upper, :size],
            dst_ref=dq_pair.at[first:upper, size:],
            send_sem=dq_send.at[index],
            recv_sem=dq_recv.at[index],
            device_id={"head": sibling},
            device_id_type=MESH,
        )
        copy.start()
        dq_copies.append(copy)

    for copy in near_copies:
        copy.wait_recv()
    dkv_copies = []
    for k in range(1, chips):
        to = lax.rem(y + k, chips)
        both = dkv_out[chip_rows(to, c), :].astype(F32) + dkv_near[to].astype(F32)
        dkv_sum[k - 1] = both.astype(BF16)
        copy = pltpu.make_async_remote_copy(
            src_ref=dkv_sum.at[k - 1],
            dst_ref=dkv_in.at[k - 1],
            send_sem=dkv_send.at[k - 1],
            recv_sem=dkv_recv.at[k - 1],
            device_id={"head": to * CORES + c},
            device_id_type=MESH,
        )
        copy.start()
        dkv_copies.append(copy)

    send_wkv(1, jnp.logical_not(early))

    def q_term(chip, b, e):
        first = pl.multiple_of(chip * CORES * tokens + e * piece, piece)
        at = pl.multiple_of(b * wide, wide)
        return dot_nt(dq_pair[pl.ds(first, piece), :], wq_pair[pl.ds(at, wide), :])

    w_copy.wait_recv()
    for copy in dq_copies:
        copy.wait_recv()
    chunks = [
        (i, core * PIECES + p)
        for i in range(per_half)
        for p in range(PIECES)
        for core in range(CORES)
    ]
    part_copies = {}

    def send_part(i, e):
        b = lax.rem(z + 1 + i, per_half)
        for k in range(1, chips):
            to = lax.rem(y + k, chips)
            part_out[k - 1, i, e] = q_term(to, b, e).astype(BF16)
            copy = pltpu.make_async_remote_copy(
                src_ref=part_out.at[k - 1, i, e],
                dst_ref=part_in.at[k - 1, i, e],
                send_sem=part_send.at[k - 1, i, e],
                recv_sem=part_recv.at[k - 1, i, e],
                device_id={"head": to * CORES + c},
                device_id_type=MESH,
            )
            copy.start()
            part_copies[k, i, e] = copy

    for i, e in chunks[:AHEAD]:
        send_part(i, e)

    total = dkv_out[chip_rows(y, c), :].astype(F32) + dkv_near[y].astype(F32)
    for k in range(1, chips):
        dkv_copies[k - 1].wait_recv()
        total = total + dkv_in[k - 1].astype(F32)
    kvg = total.astype(BF16)
    kvg_ref[...] = kvg
    kvg_pair[c] = kvg
    kvg_copy = pltpu.make_async_remote_copy(
        src_ref=kvg_pair.at[c],
        dst_ref=kvg_pair.at[c],
        send_sem=kvg_sem.at[0],
        recv_sem=kvg_sem.at[1],
        device_id={"head": sibling},
        device_id_type=MESH,
    )
    kvg_copy.start()
    pltpu.make_async_remote_copy(
        src_ref=kvg_pair.at[c],
        dst_ref=kvg_pair.at[1 - c],
        send_sem=kvg_sem.at[0],
        recv_sem=kvg_sem.at[1],
        device_id={"head": sibling},
        device_id_type=MESH,
    ).wait_recv()

    def z_copy(i, e, to_z):
        return pltpu.make_async_remote_copy(
            src_ref=z_out.at[i, e],
            dst_ref=z_in.at[z, e % PIECES],
            send_sem=z_send.at[i, e],
            recv_sem=z_recv.at[z, e % PIECES],
            device_id={"group": to_z, "head": y * CORES + e // PIECES},
            device_id_type=MESH,
        )

    for n, (i, e) in enumerate(chunks):
        b = lax.rem(z + 1 + i, per_half)
        to_z = c * per_half + b
        at = pl.multiple_of(b * wide, wide)
        if n % (CORES * PIECES) == 0:
            for s in range(owners):

                @pl.when(jnp.logical_and(c * owners + s != h, (s * rows) // wide == b))
                def _():
                    for part in range(2):
                        cut = rows // 2
                        pltpu.make_async_remote_copy(
                            src_ref=wkv_out.at[pl.ds(part * cut, cut)],
                            dst_ref=wkv_half.at[pl.ds(s * rows + part * cut, cut)],
                            send_sem=wkv_send.at[s, part],
                            recv_sem=wkv_recv.at[s, part],
                            device_id={"head": sibling},
                            device_id_type=MESH,
                        ).wait_recv()

        acc = q_term(y, b, e)
        kvg_piece = kvg_pair[e // PIECES, pl.ds(e % PIECES * piece, piece), :]
        acc = acc + dot_nt(kvg_piece, wkv_half[pl.ds(at, wide), :])
        for k in range(1, chips):
            part_copies[k, i, e].wait_recv()
            acc = acc + part_in[k - 1, i, e].astype(F32)
        z_out[i, e] = acc.astype(BF16)
        away = jnp.logical_or(to_z != z, e // PIECES != c)

        @pl.when(away)
        def _():
            z_copy(i, e, to_z).start()

        @pl.when(jnp.logical_not(away))
        def _():
            z_in[z, e % PIECES] = z_out[i, e]

        if n + AHEAD < len(chunks):
            for k in range(1, chips):
                part_copies[k, i, e].wait_send()
            send_part(*chunks[n + AHEAD])

    source_core = z // per_half
    for p in range(PIECES):
        result = None
        for source in range(groups):

            @pl.when(jnp.logical_or(source != z, source_core != c))
            def _():
                pltpu.make_async_remote_copy(
                    src_ref=z_out.at[0, 0],
                    dst_ref=z_in.at[source, p],
                    send_sem=z_send.at[0, 0],
                    recv_sem=z_recv.at[source, p],
                    device_id={"head": sibling},
                    device_id_type=MESH,
                ).wait_recv()

            term = z_in[source, p].astype(F32)
            result = term if result is None else result + term
        out_ref[p * piece : (p + 1) * piece, :] = result.astype(BF16)

    for j in range(owners):

        @pl.when(CORES * j + my_half != h)
        def _():
            wkv_copy(j, 0).wait_send()
            wkv_copy(j, 1).wait_send()

    for copy in [w_copy, *dq_copies, kvg_copy, *near_copies, *dkv_copies]:
        copy.wait_send()
    for i, e in chunks[-AHEAD:]:
        for k in range(1, chips):
            part_copies[k, i, e].wait_send()
    for i, e in chunks:
        to_z = c * per_half + lax.rem(z + 1 + i, per_half)

        @pl.when(jnp.logical_or(to_z != z, e // PIECES != c))
        def _():
            z_copy(i, e, to_z).wait_send()


def shards(groups, heads, *args):
    query, kv, q_weight, kv_weight = args[0], args[2], args[6], args[8]
    seq, size = query.shape
    model = q_weight.shape[0]
    chips = heads // CORES
    tokens = seq // heads
    piece = tokens // PIECES
    wide = model // groups
    half = model // CORES
    per_half = groups // CORES
    owners = heads // CORES
    dma = pltpu.SemaphoreType.DMA
    vmem = pl.BlockSpec(memory_space=pltpu.VMEM)
    return pl.pallas_call(
        functools.partial(kernel, groups, heads),
        out_shape=(
            pltpu.VMEM((tokens, wide), BF16),
            pltpu.VMEM((tokens, 2 * size), BF16),
        ),
        in_specs=[pl.BlockSpec(memory_space=pltpu.HBM)] * ARGS,
        out_specs=(vmem, vmem),
        scratch_shapes=[pltpu.VMEM(arg.shape, arg.dtype) for arg in args]
        + [
            dma((ARGS,)),
            pltpu.VMEM((half, 2 * size), BF16),
            pltpu.VMEM((half, size), BF16),
            pltpu.VMEM((half, 2 * size), BF16),
            pltpu.VMEM(kv_weight.shape, BF16),
            pltpu.VMEM((seq, 2 * size), BF16),
            pltpu.VMEM((seq, 2 * size), BF16),
            pltpu.VMEM((chips, tokens, 2 * size), BF16),
            pltpu.VMEM((chips - 1, tokens, 2 * size), BF16),
            pltpu.VMEM((chips - 1, tokens, 2 * size), BF16),
            pltpu.VMEM((CORES, tokens, 2 * size), BF16),
            pltpu.VMEM((chips - 1, per_half, CORES * PIECES, piece, wide), BF16),
            pltpu.VMEM((chips - 1, per_half, CORES * PIECES, piece, wide), BF16),
            pltpu.VMEM((per_half, CORES * PIECES, piece, wide), BF16),
            pltpu.VMEM((groups, PIECES, piece, wide), BF16),
            pltpu.VMEM((seq, size), F32),
            pltpu.VMEM((seq, size), F32),
            dma((2,)),
            dma((owners, 2)),
            dma((owners, 2)),
            dma((chips,)),
            dma((chips,)),
            dma((chips,)),
            dma((chips,)),
            dma((chips - 1,)),
            dma((chips - 1,)),
            dma((2,)),
            dma((chips - 1, per_half, CORES * PIECES)),
            dma((chips - 1, per_half, CORES * PIECES)),
            dma((per_half, CORES * PIECES)),
            dma((groups, PIECES)),
        ],
        compiler_params=pltpu.CompilerParams(
            collective_id=0, has_side_effects=True, vmem_limit_bytes=55 * 1024 * 1024
        ),
    )(*args)


def solution(mesh):
    return jax.shard_map(
        functools.partial(shards, mesh.shape["group"], mesh.shape["head"]),
        mesh=mesh,
        in_specs=(
            P("dp", ("group", "head")),
            P(("group", "head"), "dp"),
            P("dp", "group"),
            P("group", "dp"),
            P("dp", ("group", "head")),
            P(("group", "head"), "dp"),
            P("dp", ("group", "head")),
            P("dp", ("group", "head")),
            P(("dp", "head"), "group"),
            P(("dp", "head"), "group"),
        ),
        out_specs=(P(("dp", "head"), "group"), P(("dp", "head"), "group")),
        check_vma=False,
    )
```

```python
import functools

import jax
import jax.numpy as jnp
from jax import lax
from jax.experimental import pallas as pl
from jax.experimental.pallas import tpu as pltpu
from jax.sharding import PartitionSpec as P

MESH = pl.DeviceIdType.MESH
F32 = jnp.float32
BF16 = jnp.bfloat16
CORES = 2
BLOCK = 32
LOG2_E = 1.4426950408889634
ARGS = 10
PIECES = 4
AHEAD = 8
LOAD_ORDER = (8, 9, 6, 7, 0, 1, 2, 3, 4, 5)


def power_of_two(exponent):
    scale = jnp.where(exponent == 0, 1.0, 0.0)
    for level in (-4, -3, -2, -1, 1, 2, 3, 4):
        scale = jnp.where(exponent == level, 2.0**level, scale)
    return scale.astype(F32)


def dequant_rows(mantissa, exponent):
    blocks, rows = exponent.shape
    scale = jnp.broadcast_to(power_of_two(exponent)[:, None, :], (blocks, BLOCK, rows))
    scale = scale.reshape(blocks * BLOCK, rows).T
    return (mantissa.astype(F32) * scale).astype(BF16)


def dequant_cols(mantissa, exponent):
    blocks, columns = exponent.shape
    scale = jnp.broadcast_to(power_of_two(exponent)[:, None, :], (blocks, BLOCK, columns))
    return (mantissa.astype(F32) * scale.reshape(blocks * BLOCK, columns)).astype(BF16)


def dot_nt(a, b):
    return lax.dot_general(a, b, (((1,), (1,)), ((), ())), preferred_element_type=F32)


def dot_tn(a, b):
    return lax.dot_general(a, b, (((0,), (0,)), ((), ())), preferred_element_type=F32)


def kernel(
    groups,
    heads,
    *refs,
):
    sources, (out_ref, kvg_ref) = refs[:ARGS], refs[ARGS : ARGS + 2]
    held = refs[ARGS + 2 : 2 * ARGS + 2]
    q_ref, qe_ref, kv_ref, kve_ref, do_ref, doe_ref, wq_ref, wqe_ref, wkv_ref, wkve_ref = held
    (
        load_sem,
        wq_pair,
        wq_out,
        wkv_half,
        wkv_out,
        dq_pair,
        dkv_out,
        dkv_near,
        dkv_sum,
        dkv_in,
        kvg_pair,
        part_out,
        part_in,
        z_out,
        z_in,
        dk_acc,
        dv_acc,
        w_sem,
        wkv_send,
        wkv_recv,
        dq_send,
        dq_recv,
        near_send,
        near_recv,
        dkv_send,
        dkv_recv,
        kvg_sem,
        part_send,
        part_recv,
        z_send,
        z_recv,
    ) = refs[2 * ARGS + 2 :]
    seq, size = q_ref.shape
    model = wq_ref.shape[0]
    chips = heads // CORES
    tokens = seq // heads
    wide = model // groups
    half = model // CORES
    per_half = groups // CORES
    piece = tokens // PIECES
    rows = wkv_ref.shape[0]
    owners = heads // CORES
    scale = 1.0 / size**0.5

    z = lax.axis_index("group")
    h = lax.axis_index("head")
    y = h // CORES
    c = lax.rem(h, CORES)
    sibling = y * CORES + (1 - c)

    loads = [
        pltpu.make_async_copy(source, held[at], load_sem.at[at])
        for at, source in enumerate(sources)
    ]
    for at in LOAD_ORDER:
        loads[at].start()

    barrier = pltpu.get_barrier_semaphore()
    for k in range(1, heads):
        pl.semaphore_signal(
            barrier, inc=1, device_id={"head": lax.rem(h + k, heads)}, device_id_type=MESH
        )
    for k in range(1, groups):
        for core in range(CORES):
            pl.semaphore_signal(
                barrier,
                inc=1,
                device_id={"group": lax.rem(z + k, groups), "head": y * CORES + core},
                device_id_type=MESH,
            )

    def weight_rows(which):
        first = pl.multiple_of(which * half, half)
        first_e = pl.multiple_of(which * (half // BLOCK), half // BLOCK)
        return dequant_cols(
            wq_ref[pl.ds(first, half), :], wqe_ref[pl.ds(first_e, half // BLOCK), :]
        )

    for at in LOAD_ORDER[:2]:
        loads[at].wait()
    wkv_out[...] = dequant_cols(wkv_ref[...], wkve_ref[...])
    pl.semaphore_wait(barrier, heads - 1 + CORES * (groups - 1))

    my_half = h // owners
    my_owner = lax.rem(h, owners)
    my_slot = pl.multiple_of(my_owner * rows, rows)
    early = (my_owner * rows) // wide == lax.rem(z + 1, per_half)

    def wkv_copy(j, part):
        cut = rows // 2
        at = pl.multiple_of(my_owner * rows + part * cut, cut)
        return pltpu.make_async_remote_copy(
            src_ref=wkv_out.at[pl.ds(part * cut, cut)],
            dst_ref=wkv_half.at[pl.ds(at, cut)],
            send_sem=wkv_send.at[j, part],
            recv_sem=wkv_recv.at[my_owner, part],
            device_id={"head": CORES * j + my_half},
            device_id_type=MESH,
        )

    def send_wkv(part, now):
        for j in range(owners):

            @pl.when(jnp.logical_and(CORES * j + my_half != h, now))
            def _():
                wkv_copy(j, part).start()

    send_wkv(0, True)
    send_wkv(1, early)

    for at in LOAD_ORDER[2:4]:
        loads[at].wait()
    wq_out[...] = weight_rows(1 - c)
    w_copy = pltpu.make_async_remote_copy(
        src_ref=wq_out,
        dst_ref=wq_pair.at[:, size:],
        send_sem=w_sem.at[0],
        recv_sem=w_sem.at[1],
        device_id={"head": sibling},
        device_id_type=MESH,
    )
    w_copy.start()
    wq_pair[:, :size] = weight_rows(c)

    @pl.when(my_half == c)
    def _():
        wkv_half[pl.ds(my_slot, rows), :] = wkv_out[...]

    for at in LOAD_ORDER[4:]:
        loads[at].wait()
    query = dequant_rows(q_ref[...], qe_ref[...])
    kv = dequant_rows(kv_ref[...], kve_ref[...])
    grad = dequant_rows(do_ref[...], doe_ref[...])
    keys, values = kv[:, :size], kv[:, size:]
    block = CORES * tokens
    visible = lax.broadcasted_iota(jnp.int32, (block, block), 0) <= lax.broadcasted_iota(
        jnp.int32, (block, block), 1
    )
    dq_copies, near_copies = [], []

    def chip_rows(chip, core):
        return pl.ds(pl.multiple_of((chip * CORES + core) * tokens, tokens), tokens)

    for index in reversed(range(chips)):
        first, upper = index * block, (index + 1) * block
        q_block, do_block = query[first:upper], grad[first:upper]
        spans = [(first, upper)] + ([(0, first)] if first else [])
        scores = [dot_nt(keys[lo:hi], q_block) for lo, hi in spans]
        scores[0] = jnp.where(visible, scores[0], -jnp.inf)
        peak = functools.reduce(
            jnp.maximum, [jnp.max(part, axis=0, keepdims=True) for part in scores]
        )
        expd = [jnp.exp2((part - peak) * (scale * LOG2_E)) for part in scores]
        total = sum(jnp.sum(part, axis=0, keepdims=True) for part in expd)
        inverse = 1.0 / total
        probs = [part * inverse for part in expd]
        dprob = [dot_nt(values[lo:hi], do_block) for lo, hi in spans]
        delta = sum(
            jnp.sum(p * dp, axis=0, keepdims=True) for p, dp in zip(probs, dprob)
        )
        dscore = [(p * (dp - delta)).astype(BF16) for p, dp in zip(probs, dprob)]
        for part, p, (lo, hi) in zip(dscore, probs, spans):
            dk = jnp.dot(part, q_block, preferred_element_type=F32)
            dv = jnp.dot(p.astype(BF16), do_block, preferred_element_type=F32)
            if upper == seq:
                dk_acc[lo:hi, :] = dk
                dv_acc[lo:hi, :] = dv
            else:
                dk_acc[lo:hi, :] += dk
                dv_acc[lo:hi, :] += dv

        dkv_out[first:upper, :size] = (dk_acc[first:upper, :] * scale).astype(BF16)
        dkv_out[first:upper, size:] = dv_acc[first:upper, :].astype(BF16)
        copy = pltpu.make_async_remote_copy(
            src_ref=dkv_out.at[chip_rows(index, 1 - c)],
            dst_ref=dkv_near.at[index],
            send_sem=near_send.at[index],
            recv_sem=near_recv.at[index],
            device_id={"head": sibling},
            device_id_type=MESH,
        )
        copy.start()
        near_copies.append(copy)
        dq = sum(dot_tn(part, keys[lo:hi]) for part, (lo, hi) in zip(dscore, spans))
        dq_pair[first:upper, :size] = (dq * scale).astype(BF16)
        copy = pltpu.make_async_remote_copy(
            src_ref=dq_pair.at[first:upper, :size],
            dst_ref=dq_pair.at[first:upper, size:],
            send_sem=dq_send.at[index],
            recv_sem=dq_recv.at[index],
            device_id={"head": sibling},
            device_id_type=MESH,
        )
        copy.start()
        dq_copies.append(copy)

    for copy in near_copies:
        copy.wait_recv()
    dkv_copies = []
    for k in range(1, chips):
        to = lax.rem(y + k, chips)
        both = dkv_out[chip_rows(to, c), :].astype(F32) + dkv_near[to].astype(F32)
        dkv_sum[k - 1] = both.astype(BF16)
        copy = pltpu.make_async_remote_copy(
            src_ref=dkv_sum.at[k - 1],
            dst_ref=dkv_in.at[k - 1],
            send_sem=dkv_send.at[k - 1],
            recv_sem=dkv_recv.at[k - 1],
            device_id={"head": to * CORES + c},
            device_id_type=MESH,
        )
        copy.start()
        dkv_copies.append(copy)

    send_wkv(1, jnp.logical_not(early))

    def q_term(chip, b, e):
        first = pl.multiple_of(chip * CORES * tokens + e * piece, piece)
        at = pl.multiple_of(b * wide, wide)
        return dot_nt(dq_pair[pl.ds(first, piece), :], wq_pair[pl.ds(at, wide), :])

    w_copy.wait_recv()
    for copy in dq_copies:
        copy.wait_recv()
    chunks = [
        (i, core * PIECES + p)
        for i in range(per_half)
        for p in range(PIECES)
        for core in range(CORES)
    ]
    part_copies = {}

    def send_part(i, e):
        b = lax.rem(z + 1 + i, per_half)
        for k in range(1, chips):
            to = lax.rem(y + k, chips)
            part_out[k - 1, i, e] = q_term(to, b, e).astype(BF16)
            copy = pltpu.make_async_remote_copy(
                src_ref=part_out.at[k - 1, i, e],
                dst_ref=part_in.at[k - 1, i, e],
                send_sem=part_send.at[k - 1, i, e],
                recv_sem=part_recv.at[k - 1, i, e],
                device_id={"head": to * CORES + c},
                device_id_type=MESH,
            )
            copy.start()
            part_copies[k, i, e] = copy

    for i, e in chunks[:AHEAD]:
        send_part(i, e)

    total = dkv_out[chip_rows(y, c), :].astype(F32) + dkv_near[y].astype(F32)
    for k in range(1, chips):
        dkv_copies[k - 1].wait_recv()
        total = total + dkv_in[k - 1].astype(F32)
    kvg = total.astype(BF16)
    kvg_ref[...] = kvg
    kvg_pair[c] = kvg
    kvg_copy = pltpu.make_async_remote_copy(
        src_ref=kvg_pair.at[c],
        dst_ref=kvg_pair.at[c],
        send_sem=kvg_sem.at[0],
        recv_sem=kvg_sem.at[1],
        device_id={"head": sibling},
        device_id_type=MESH,
    )
    kvg_copy.start()
    pltpu.make_async_remote_copy(
        src_ref=kvg_pair.at[c],
        dst_ref=kvg_pair.at[1 - c],
        send_sem=kvg_sem.at[0],
        recv_sem=kvg_sem.at[1],
        device_id={"head": sibling},
        device_id_type=MESH,
    ).wait_recv()

    def z_copy(i, e, to_z):
        return pltpu.make_async_remote_copy(
            src_ref=z_out.at[i, e],
            dst_ref=z_in.at[z, e % PIECES],
            send_sem=z_send.at[i, e],
            recv_sem=z_recv.at[z, e % PIECES],
            device_id={"group": to_z, "head": y * CORES + e // PIECES},
            device_id_type=MESH,
        )

    for n, (i, e) in enumerate(chunks):
        b = lax.rem(z + 1 + i, per_half)
        to_z = c * per_half + b
        at = pl.multiple_of(b * wide, wide)
        if n % (CORES * PIECES) == 0:
            for s in range(owners):

                @pl.when(jnp.logical_and(c * owners + s != h, (s * rows) // wide == b))
                def _():
                    for part in range(2):
                        cut = rows // 2
                        pltpu.make_async_remote_copy(
                            src_ref=wkv_out.at[pl.ds(part * cut, cut)],
                            dst_ref=wkv_half.at[pl.ds(s * rows + part * cut, cut)],
                            send_sem=wkv_send.at[s, part],
                            recv_sem=wkv_recv.at[s, part],
                            device_id={"head": sibling},
                            device_id_type=MESH,
                        ).wait_recv()

        acc = q_term(y, b, e)
        kvg_piece = kvg_pair[e // PIECES, pl.ds(e % PIECES * piece, piece), :]
        acc = acc + dot_nt(kvg_piece, wkv_half[pl.ds(at, wide), :])
        for k in range(1, chips):
            part_copies[k, i, e].wait_recv()
            acc = acc + part_in[k - 1, i, e].astype(F32)
        z_out[i, e] = acc.astype(BF16)
        away = jnp.logical_or(to_z != z, e // PIECES != c)

        @pl.when(away)
        def _():
            z_copy(i, e, to_z).start()

        @pl.when(jnp.logical_not(away))
        def _():
            z_in[z, e % PIECES] = z_out[i, e]

        if n + AHEAD < len(chunks):
            for k in range(1, chips):
                part_copies[k, i, e].wait_send()
            send_part(*chunks[n + AHEAD])

    source_core = z // per_half
    for p in range(PIECES):
        result = None
        for source in range(groups):

            @pl.when(jnp.logical_or(source != z, source_core != c))
            def _():
                pltpu.make_async_remote_copy(
                    src_ref=z_out.at[0, 0],
                    dst_ref=z_in.at[source, p],
                    send_sem=z_send.at[0, 0],
                    recv_sem=z_recv.at[source, p],
                    device_id={"head": sibling},
                    device_id_type=MESH,
                ).wait_recv()

            term = z_in[source, p].astype(F32)
            result = term if result is None else result + term
        out_ref[p * piece : (p + 1) * piece, :] = result.astype(BF16)

    for j in range(owners):

        @pl.when(CORES * j + my_half != h)
        def _():
            wkv_copy(j, 0).wait_send()
            wkv_copy(j, 1).wait_send()

    for copy in [w_copy, *dq_copies, kvg_copy, *near_copies, *dkv_copies]:
        copy.wait_send()
    for i, e in chunks[-AHEAD:]:
        for k in range(1, chips):
            part_copies[k, i, e].wait_send()
    for i, e in chunks:
        to_z = c * per_half + lax.rem(z + 1 + i, per_half)

        @pl.when(jnp.logical_or(to_z != z, e // PIECES != c))
        def _():
            z_copy(i, e, to_z).wait_send()


def shards(groups, heads, *args):
    query, kv, q_weight, kv_weight = args[0], args[2], args[6], args[8]
    seq, size = query.shape
    model = q_weight.shape[0]
    chips = heads // CORES
    tokens = seq // heads
    piece = tokens // PIECES
    wide = model // groups
    half = model // CORES
    per_half = groups // CORES
    owners = heads // CORES
    dma = pltpu.SemaphoreType.DMA
    vmem = pl.BlockSpec(memory_space=pltpu.VMEM)
    return pl.pallas_call(
        functools.partial(kernel, groups, heads),
        out_shape=(
            pltpu.VMEM((tokens, wide), BF16),
            pltpu.VMEM((tokens, 2 * size), BF16),
        ),
        in_specs=[pl.BlockSpec(memory_space=pltpu.HBM)] * ARGS,
        out_specs=(vmem, vmem),
        scratch_shapes=[pltpu.VMEM(arg.shape, arg.dtype) for arg in args]
        + [
            dma((ARGS,)),
            pltpu.VMEM((half, 2 * size), BF16),
            pltpu.VMEM((half, size), BF16),
            pltpu.VMEM((half, 2 * size), BF16),
            pltpu.VMEM(kv_weight.shape, BF16),
            pltpu.VMEM((seq, 2 * size), BF16),
            pltpu.VMEM((seq, 2 * size), BF16),
            pltpu.VMEM((chips, tokens, 2 * size), BF16),
            pltpu.VMEM((chips - 1, tokens, 2 * size), BF16),
            pltpu.VMEM((chips - 1, tokens, 2 * size), BF16),
            pltpu.VMEM((CORES, tokens, 2 * size), BF16),
            pltpu.VMEM((chips - 1, per_half, CORES * PIECES, piece, wide), BF16),
            pltpu.VMEM((chips - 1, per_half, CORES * PIECES, piece, wide), BF16),
            pltpu.VMEM((per_half, CORES * PIECES, piece, wide), BF16),
            pltpu.VMEM((groups, PIECES, piece, wide), BF16),
            pltpu.VMEM((seq, size), F32),
            pltpu.VMEM((seq, size), F32),
            dma((2,)),
            dma((owners, 2)),
            dma((owners, 2)),
            dma((chips,)),
            dma((chips,)),
            dma((chips,)),
            dma((chips,)),
            dma((chips - 1,)),
            dma((chips - 1,)),
            dma((2,)),
            dma((chips - 1, per_half, CORES * PIECES)),
            dma((chips - 1, per_half, CORES * PIECES)),
            dma((per_half, CORES * PIECES)),
            dma((groups, PIECES)),
        ],
        compiler_params=pltpu.CompilerParams(
            collective_id=0, has_side_effects=True, vmem_limit_bytes=55 * 1024 * 1024
        ),
    )(*args)


def solution(mesh):
    return jax.shard_map(
        functools.partial(shards, mesh.shape["group"], mesh.shape["head"]),
        mesh=mesh,
        in_specs=(
            P("dp", ("group", "head")),
            P(("group", "head"), "dp"),
            P("dp", "group"),
            P("group", "dp"),
            P("dp", ("group", "head")),
            P(("group", "head"), "dp"),
            P("dp", ("group", "head")),
            P("dp", ("group", "head")),
            P(("dp", "head"), "group"),
            P(("dp", "head"), "group"),
        ),
        out_specs=(P(("dp", "head"), "group"), P(("dp", "head"), "group")),
        check_vma=False,
    )
```

```python
import functools

import jax
import jax.numpy as jnp
from jax import lax
from jax.experimental import pallas as pl
from jax.experimental.pallas import tpu as pltpu
from jax.sharding import PartitionSpec as P

MESH = pl.DeviceIdType.MESH
F32 = jnp.float32
BF16 = jnp.bfloat16
CORES = 2
BLOCK = 32
LOG2_E = 1.4426950408889634
ARGS = 10
PIECES = 2
AHEAD = 4
LOAD_ORDER = (8, 9, 6, 7, 0, 1, 2, 3, 4, 5)


def power_of_two(exponent):
    scale = jnp.where(exponent == 0, 1.0, 0.0)
    for level in (-4, -3, -2, -1, 1, 2, 3, 4):
        scale = jnp.where(exponent == level, 2.0**level, scale)
    return scale.astype(F32)


def dequant_rows(mantissa, exponent):
    blocks, rows = exponent.shape
    scale = jnp.broadcast_to(power_of_two(exponent)[:, None, :], (blocks, BLOCK, rows))
    scale = scale.reshape(blocks * BLOCK, rows).T
    return (mantissa.astype(F32) * scale).astype(BF16)


def dequant_cols(mantissa, exponent):
    blocks, columns = exponent.shape
    scale = jnp.broadcast_to(power_of_two(exponent)[:, None, :], (blocks, BLOCK, columns))
    return (mantissa.astype(F32) * scale.reshape(blocks * BLOCK, columns)).astype(BF16)


def dot_nt(a, b):
    return lax.dot_general(a, b, (((1,), (1,)), ((), ())), preferred_element_type=F32)


def dot_tn(a, b):
    return lax.dot_general(a, b, (((0,), (0,)), ((), ())), preferred_element_type=F32)


def kernel(
    groups,
    heads,
    *refs,
):
    sources, (out_ref, kvg_ref) = refs[:ARGS], refs[ARGS : ARGS + 2]
    held = refs[ARGS + 2 : 2 * ARGS + 2]
    q_ref, qe_ref, kv_ref, kve_ref, do_ref, doe_ref, wq_ref, wqe_ref, wkv_ref, wkve_ref = held
    (
        load_sem,
        wq_pair,
        wq_out,
        wkv_half,
        wkv_out,
        dq_pair,
        dkv_out,
        dkv_near,
        dkv_sum,
        dkv_in,
        kvg_pair,
        part_out,
        part_in,
        z_out,
        z_in,
        dk_acc,
        dv_acc,
        w_sem,
        wkv_send,
        wkv_recv,
        dq_send,
        dq_recv,
        near_send,
        near_recv,
        dkv_send,
        dkv_recv,
        kvg_sem,
        part_send,
        part_recv,
        z_send,
        z_recv,
    ) = refs[2 * ARGS + 2 :]
    seq, size = q_ref.shape
    model = wq_ref.shape[0]
    chips = heads // CORES
    tokens = seq // heads
    wide = model // groups
    half = model // CORES
    per_half = groups // CORES
    piece = tokens // PIECES
    rows = wkv_ref.shape[0]
    owners = heads // CORES
    scale = 1.0 / size**0.5

    z = lax.axis_index("group")
    h = lax.axis_index("head")
    y = h // CORES
    c = lax.rem(h, CORES)
    sibling = y * CORES + (1 - c)

    loads = [
        pltpu.make_async_copy(source, held[at], load_sem.at[at])
        for at, source in enumerate(sources)
    ]
    for at in LOAD_ORDER:
        loads[at].start()

    barrier = pltpu.get_barrier_semaphore()
    for k in range(1, heads):
        pl.semaphore_signal(
            barrier, inc=1, device_id={"head": lax.rem(h + k, heads)}, device_id_type=MESH
        )
    for k in range(1, groups):
        for core in range(CORES):
            pl.semaphore_signal(
                barrier,
                inc=1,
                device_id={"group": lax.rem(z + k, groups), "head": y * CORES + core},
                device_id_type=MESH,
            )

    def weight_rows(which):
        first = pl.multiple_of(which * half, half)
        first_e = pl.multiple_of(which * (half // BLOCK), half // BLOCK)
        return dequant_cols(
            wq_ref[pl.ds(first, half), :], wqe_ref[pl.ds(first_e, half // BLOCK), :]
        )

    for at in LOAD_ORDER[:2]:
        loads[at].wait()
    wkv_out[...] = dequant_cols(wkv_ref[...], wkve_ref[...])
    pl.semaphore_wait(barrier, heads - 1 + CORES * (groups - 1))

    my_half = h // owners
    my_owner = lax.rem(h, owners)
    my_slot = pl.multiple_of(my_owner * rows, rows)
    early = (my_owner * rows) // wide == lax.rem(z + 1, per_half)

    def wkv_copy(j, part):
        cut = rows // 2
        at = pl.multiple_of(my_owner * rows + part * cut, cut)
        return pltpu.make_async_remote_copy(
            src_ref=wkv_out.at[pl.ds(part * cut, cut)],
            dst_ref=wkv_half.at[pl.ds(at, cut)],
            send_sem=wkv_send.at[j, part],
            recv_sem=wkv_recv.at[my_owner, part],
            device_id={"head": CORES * j + my_half},
            device_id_type=MESH,
        )

    def send_wkv(part, now):
        for j in range(owners):

            @pl.when(jnp.logical_and(CORES * j + my_half != h, now))
            def _():
                wkv_copy(j, part).start()

    send_wkv(0, True)
    send_wkv(1, early)

    for at in LOAD_ORDER[2:4]:
        loads[at].wait()
    wq_out[...] = weight_rows(1 - c)
    w_copy = pltpu.make_async_remote_copy(
        src_ref=wq_out,
        dst_ref=wq_pair.at[:, size:],
        send_sem=w_sem.at[0],
        recv_sem=w_sem.at[1],
        device_id={"head": sibling},
        device_id_type=MESH,
    )
    w_copy.start()
    wq_pair[:, :size] = weight_rows(c)

    @pl.when(my_half == c)
    def _():
        wkv_half[pl.ds(my_slot, rows), :] = wkv_out[...]

    for at in LOAD_ORDER[4:]:
        loads[at].wait()
    query = dequant_rows(q_ref[...], qe_ref[...])
    kv = dequant_rows(kv_ref[...], kve_ref[...])
    grad = dequant_rows(do_ref[...], doe_ref[...])
    keys, values = kv[:, :size], kv[:, size:]
    block = CORES * tokens
    visible = lax.broadcasted_iota(jnp.int32, (block, block), 0) <= lax.broadcasted_iota(
        jnp.int32, (block, block), 1
    )
    dq_copies, near_copies = [], []

    def chip_rows(chip, core):
        return pl.ds(pl.multiple_of((chip * CORES + core) * tokens, tokens), tokens)

    for index in reversed(range(chips)):
        first, upper = index * block, (index + 1) * block
        q_block, do_block = query[first:upper], grad[first:upper]
        spans = [(first, upper)] + ([(0, first)] if first else [])
        scores = [dot_nt(keys[lo:hi], q_block) for lo, hi in spans]
        scores[0] = jnp.where(visible, scores[0], -jnp.inf)
        peak = functools.reduce(
            jnp.maximum, [jnp.max(part, axis=0, keepdims=True) for part in scores]
        )
        expd = [jnp.exp2((part - peak) * (scale * LOG2_E)) for part in scores]
        total = sum(jnp.sum(part, axis=0, keepdims=True) for part in expd)
        inverse = 1.0 / total
        probs = [part * inverse for part in expd]
        dprob = [dot_nt(values[lo:hi], do_block) for lo, hi in spans]
        delta = sum(
            jnp.sum(p * dp, axis=0, keepdims=True) for p, dp in zip(probs, dprob)
        )
        dscore = [(p * (dp - delta)).astype(BF16) for p, dp in zip(probs, dprob)]
        for part, p, (lo, hi) in zip(dscore, probs, spans):
            dk = jnp.dot(part, q_block, preferred_element_type=F32)
            dv = jnp.dot(p.astype(BF16), do_block, preferred_element_type=F32)
            if upper == seq:
                dk_acc[lo:hi, :] = dk
                dv_acc[lo:hi, :] = dv
            else:
                dk_acc[lo:hi, :] += dk
                dv_acc[lo:hi, :] += dv

        dkv_out[first:upper, :size] = (dk_acc[first:upper, :] * scale).astype(BF16)
        dkv_out[first:upper, size:] = dv_acc[first:upper, :].astype(BF16)
        copy = pltpu.make_async_remote_copy(
            src_ref=dkv_out.at[chip_rows(index, 1 - c)],
            dst_ref=dkv_near.at[index],
            send_sem=near_send.at[index],
            recv_sem=near_recv.at[index],
            device_id={"head": sibling},
            device_id_type=MESH,
        )
        copy.start()
        near_copies.append(copy)
        dq = sum(dot_tn(part, keys[lo:hi]) for part, (lo, hi) in zip(dscore, spans))
        dq_pair[first:upper, :size] = (dq * scale).astype(BF16)
        copy = pltpu.make_async_remote_copy(
            src_ref=dq_pair.at[first:upper, :size],
            dst_ref=dq_pair.at[first:upper, size:],
            send_sem=dq_send.at[index],
            recv_sem=dq_recv.at[index],
            device_id={"head": sibling},
            device_id_type=MESH,
        )
        copy.start()
        dq_copies.append(copy)

    for copy in near_copies:
        copy.wait_recv()
    dkv_copies = []
    for k in range(1, chips):
        to = lax.rem(y + k, chips)
        both = dkv_out[chip_rows(to, c), :].astype(F32) + dkv_near[to].astype(F32)
        dkv_sum[k - 1] = both.astype(BF16)
        copy = pltpu.make_async_remote_copy(
            src_ref=dkv_sum.at[k - 1],
            dst_ref=dkv_in.at[k - 1],
            send_sem=dkv_send.at[k - 1],
            recv_sem=dkv_recv.at[k - 1],
            device_id={"head": to * CORES + c},
            device_id_type=MESH,
        )
        copy.start()
        dkv_copies.append(copy)

    def q_term(chip, b, e):
        first = pl.multiple_of(chip * CORES * tokens + e * piece, piece)
        at = pl.multiple_of(b * wide, wide)
        return dot_nt(dq_pair[pl.ds(first, piece), :], wq_pair[pl.ds(at, wide), :])

    w_copy.wait_recv()
    for copy in dq_copies:
        copy.wait_recv()
    chunks = [
        (i, core * PIECES + p)
        for i in range(per_half)
        for p in range(PIECES)
        for core in range(CORES)
    ]
    part_copies = {}

    def send_part(i, e):
        b = lax.rem(z + 1 + i, per_half)
        for k in range(1, chips):
            to = lax.rem(y + k, chips)
            part_out[k - 1, i, e] = q_term(to, b, e).astype(BF16)
            copy = pltpu.make_async_remote_copy(
                src_ref=part_out.at[k - 1, i, e],
                dst_ref=part_in.at[k - 1, i, e],
                send_sem=part_send.at[k - 1, i, e],
                recv_sem=part_recv.at[k - 1, i, e],
                device_id={"head": to * CORES + c},
                device_id_type=MESH,
            )
            copy.start()
            part_copies[k, i, e] = copy

    for i, e in chunks[:AHEAD]:
        send_part(i, e)

    send_wkv(1, jnp.logical_not(early))

    total = dkv_out[chip_rows(y, c), :].astype(F32) + dkv_near[y].astype(F32)
    for k in range(1, chips):
        dkv_copies[k - 1].wait_recv()
        total = total + dkv_in[k - 1].astype(F32)
    kvg = total.astype(BF16)
    kvg_ref[...] = kvg
    kvg_pair[c] = kvg
    kvg_copy = pltpu.make_async_remote_copy(
        src_ref=kvg_pair.at[c],
        dst_ref=kvg_pair.at[c],
        send_sem=kvg_sem.at[0],
        recv_sem=kvg_sem.at[1],
        device_id={"head": sibling},
        device_id_type=MESH,
    )
    kvg_copy.start()
    pltpu.make_async_remote_copy(
        src_ref=kvg_pair.at[c],
        dst_ref=kvg_pair.at[1 - c],
        send_sem=kvg_sem.at[0],
        recv_sem=kvg_sem.at[1],
        device_id={"head": sibling},
        device_id_type=MESH,
    ).wait_recv()

    def z_copy(i, e, to_z):
        return pltpu.make_async_remote_copy(
            src_ref=z_out.at[i, e],
            dst_ref=z_in.at[z, e % PIECES],
            send_sem=z_send.at[i, e],
            recv_sem=z_recv.at[z, e % PIECES],
            device_id={"group": to_z, "head": y * CORES + e // PIECES},
            device_id_type=MESH,
        )

    for n, (i, e) in enumerate(chunks):
        b = lax.rem(z + 1 + i, per_half)
        to_z = c * per_half + b
        at = pl.multiple_of(b * wide, wide)
        if n % (CORES * PIECES) == 0:
            for s in range(owners):

                @pl.when(jnp.logical_and(c * owners + s != h, (s * rows) // wide == b))
                def _():
                    for part in range(2):
                        cut = rows // 2
                        pltpu.make_async_remote_copy(
                            src_ref=wkv_out.at[pl.ds(part * cut, cut)],
                            dst_ref=wkv_half.at[pl.ds(s * rows + part * cut, cut)],
                            send_sem=wkv_send.at[s, part],
                            recv_sem=wkv_recv.at[s, part],
                            device_id={"head": sibling},
                            device_id_type=MESH,
                        ).wait_recv()

        acc = q_term(y, b, e)
        kvg_piece = kvg_pair[e // PIECES, pl.ds(e % PIECES * piece, piece), :]
        acc = acc + dot_nt(kvg_piece, wkv_half[pl.ds(at, wide), :])
        for k in range(1, chips):
            part_copies[k, i, e].wait_recv()
            acc = acc + part_in[k - 1, i, e].astype(F32)
        z_out[i, e] = acc.astype(BF16)
        away = jnp.logical_or(to_z != z, e // PIECES != c)

        @pl.when(away)
        def _():
            z_copy(i, e, to_z).start()

        @pl.when(jnp.logical_not(away))
        def _():
            z_in[z, e % PIECES] = z_out[i, e]

        if n + AHEAD < len(chunks):
            for k in range(1, chips):
                part_copies[k, i, e].wait_send()
            send_part(*chunks[n + AHEAD])

    source_core = z // per_half
    for p in range(PIECES):
        result = None
        for source in range(groups):

            @pl.when(jnp.logical_or(source != z, source_core != c))
            def _():
                pltpu.make_async_remote_copy(
                    src_ref=z_out.at[0, 0],
                    dst_ref=z_in.at[source, p],
                    send_sem=z_send.at[0, 0],
                    recv_sem=z_recv.at[source, p],
                    device_id={"head": sibling},
                    device_id_type=MESH,
                ).wait_recv()

            term = z_in[source, p].astype(F32)
            result = term if result is None else result + term
        out_ref[p * piece : (p + 1) * piece, :] = result.astype(BF16)

    for j in range(owners):

        @pl.when(CORES * j + my_half != h)
        def _():
            wkv_copy(j, 0).wait_send()
            wkv_copy(j, 1).wait_send()

    for copy in [w_copy, *dq_copies, kvg_copy, *near_copies, *dkv_copies]:
        copy.wait_send()
    for i, e in chunks[-AHEAD:]:
        for k in range(1, chips):
            part_copies[k, i, e].wait_send()
    for i, e in chunks:
        to_z = c * per_half + lax.rem(z + 1 + i, per_half)

        @pl.when(jnp.logical_or(to_z != z, e // PIECES != c))
        def _():
            z_copy(i, e, to_z).wait_send()


def shards(groups, heads, *args):
    query, kv, q_weight, kv_weight = args[0], args[2], args[6], args[8]
    seq, size = query.shape
    model = q_weight.shape[0]
    chips = heads // CORES
    tokens = seq // heads
    piece = tokens // PIECES
    wide = model // groups
    half = model // CORES
    per_half = groups // CORES
    owners = heads // CORES
    dma = pltpu.SemaphoreType.DMA
    vmem = pl.BlockSpec(memory_space=pltpu.VMEM)
    return pl.pallas_call(
        functools.partial(kernel, groups, heads),
        out_shape=(
            pltpu.VMEM((tokens, wide), BF16),
            pltpu.VMEM((tokens, 2 * size), BF16),
        ),
        in_specs=[pl.BlockSpec(memory_space=pltpu.HBM)] * ARGS,
        out_specs=(vmem, vmem),
        scratch_shapes=[pltpu.VMEM(arg.shape, arg.dtype) for arg in args]
        + [
            dma((ARGS,)),
            pltpu.VMEM((half, 2 * size), BF16),
            pltpu.VMEM((half, size), BF16),
            pltpu.VMEM((half, 2 * size), BF16),
            pltpu.VMEM(kv_weight.shape, BF16),
            pltpu.VMEM((seq, 2 * size), BF16),
            pltpu.VMEM((seq, 2 * size), BF16),
            pltpu.VMEM((chips, tokens, 2 * size), BF16),
            pltpu.VMEM((chips - 1, tokens, 2 * size), BF16),
            pltpu.VMEM((chips - 1, tokens, 2 * size), BF16),
            pltpu.VMEM((CORES, tokens, 2 * size), BF16),
            pltpu.VMEM((chips - 1, per_half, CORES * PIECES, piece, wide), BF16),
            pltpu.VMEM((chips - 1, per_half, CORES * PIECES, piece, wide), BF16),
            pltpu.VMEM((per_half, CORES * PIECES, piece, wide), BF16),
            pltpu.VMEM((groups, PIECES, piece, wide), BF16),
            pltpu.VMEM((seq, size), F32),
            pltpu.VMEM((seq, size), F32),
            dma((2,)),
            dma((owners, 2)),
            dma((owners, 2)),
            dma((chips,)),
            dma((chips,)),
            dma((chips,)),
            dma((chips,)),
            dma((chips - 1,)),
            dma((chips - 1,)),
            dma((2,)),
            dma((chips - 1, per_half, CORES * PIECES)),
            dma((chips - 1, per_half, CORES * PIECES)),
            dma((per_half, CORES * PIECES)),
            dma((groups, PIECES)),
        ],
        compiler_params=pltpu.CompilerParams(
            collective_id=0, has_side_effects=True, vmem_limit_bytes=55 * 1024 * 1024
        ),
    )(*args)


def solution(mesh):
    return jax.shard_map(
        functools.partial(shards, mesh.shape["group"], mesh.shape["head"]),
        mesh=mesh,
        in_specs=(
            P("dp", ("group", "head")),
            P(("group", "head"), "dp"),
            P("dp", "group"),
            P("group", "dp"),
            P("dp", ("group", "head")),
            P(("group", "head"), "dp"),
            P("dp", ("group", "head")),
            P("dp", ("group", "head")),
            P(("dp", "head"), "group"),
            P(("dp", "head"), "group"),
        ),
        out_specs=(P(("dp", "head"), "group"), P(("dp", "head"), "group")),
        check_vma=False,
    )
```
